128 devices in a mesh: row: 8 (over z, y_hi), col: 16 (over x, y_lo, core).
Axes of the slice: x: 4, y: 4 (y_hi: 2, y_lo: 2; y = y_hi * 2 + y_lo), z: 4, core: 2. Of those that a mesh axis runs over, the one named last changes fastest.
Arguments:
- obj: float32 [2, 2048, 4096], P(None, 'row', 'col'), may hold values from -4.2 to 4.2
- probe: float32 [2, 256, 256], replicated, may hold values from -4.2 to 4.2
- amplitudes: bfloat16 [512, 256, 256], P(('row', 'col')), may hold values from 0.049804688 to 4
- positions: int32 [512, 2], replicated, may hold values from 0 to 3840, as said below
Outputs:
- new_object: float32 [2, 2048, 4096], P(None, 'row', 'col')
- new_probe: float32 [2, 256, 256], replicated
The draws below stay inside these ranges and needn't reach their ends.
Inputs may be any that keep to these rules, and one draw needn't show every extreme that they name: `positions`: entry p is the top-left cell (row, column) of pattern p's window of 256 x 256 cells, which lies inside the object. Pattern p is held by device p // 4 in row-major order of (row, col), and its row offset lies in that device's band of 256 object rows. One device holds at most 2 patterns whose window starts in one tile, and exactly 2 for some tile in every draw; at most 8 windows start in one tile, and in every row of tiles exactly 8 start in one tile.
All inputs are finite; a program needn't handle non-finite values.
Results may differ from the reference program's by a relative error of at most 0.0018.
Values may be sent and summed in bfloat16 or wider, within the bound.
A program may use at most 128 MiB of HBM per device.

```python
import math
import jax
import jax.numpy as jnp
from jax import lax

M = 256
TH = 256
TW = 256
PAT_DEV = 4
ITERS = 2
SEND = 2
CAP = 8
NY = 2048
NX = 4096
PATTERNS = 512
N_ROW = 8
N_COL = 16


def route_tables(key):
    base = jax.random.fold_in(key, 11)
    band_keys = jax.random.split(base, N_ROW)
    busy_count = CAP // SEND

    def one_band(band_key, band):
        keys = jax.random.split(band_key, 6)
        busy_owner = jax.random.randint(keys[0], (), 0, N_COL)
        source_order = jax.random.permutation(keys[1], N_COL)
        is_busy = jnp.zeros((N_COL,), jnp.int32).at[source_order[:busy_count]].set(1)
        others = jax.random.permutation(keys[2], N_COL - 1).astype(jnp.int32)
        others = others + (others >= busy_owner).astype(jnp.int32)
        drawn_count = PAT_DEV - is_busy * SEND
        first = jnp.cumsum(drawn_count) - drawn_count
        local = jnp.arange(PAT_DEV, dtype=jnp.int32)
        to_busy = (is_busy[:, None] == 1) & (local[None, :] < SEND)
        counter = first[:, None] + local[None, :] - is_busy[:, None] * SEND
        owner = jnp.where(to_busy, busy_owner, others[jnp.maximum(counter, 0) % (N_COL - 1)])
        shuffle_keys = jax.random.split(keys[3], N_COL)
        owner = jax.vmap(lambda shuffle_key, values: values[jax.random.permutation(shuffle_key, PAT_DEV)])(shuffle_keys, owner)
        y_limit = jnp.where(band == N_ROW - 1, TH - M + 1, TH)
        y_start = band * TH + jax.random.randint(keys[4], (N_COL, PAT_DEV), 0, y_limit)
        x_limit = jnp.where(owner == N_COL - 1, TW - M + 1, TW)
        x_start = owner * TW + jax.random.randint(keys[5], (N_COL, PAT_DEV), 0, x_limit)
        return (owner, y_start, x_start)
    owners, y_all, x_all = jax.vmap(one_band)(band_keys, jnp.arange(N_ROW, dtype=jnp.int32))
    positions = jnp.stack([y_all.reshape(-1), x_all.reshape(-1)], axis=-1).astype(jnp.int32)
    return positions


def draw_positions(key, part):
    return route_tables(key)


def levels(key, dims, cuts, low, largest):
    gain = 1.0
    for position, shards_of in cuts:
        steps = jax.random.uniform(jax.random.fold_in(jax.random.fold_in(key, 6), position), (shards_of,), jnp.float32, low / len(cuts), largest / len(cuts))
        gain = gain * jnp.repeat(jnp.exp(steps), dims[position] // shards_of).reshape((-1,) + (1,) * (len(dims) - 1 - position))
    return gain


def centred(key, shape, deviation, reach, shards=(), kind=jnp.bfloat16):
    entries = jax.random.normal(key, shape, jnp.float32) * deviation
    if len(shards) > 0:
        entries = levels(key, shape, shards, -0.22, 0.18) * entries
    return jnp.clip(entries, min=-reach, max=reach).astype(kind)


def setup_inputs(seed: int = 0) -> dict:
    streams_of = jax.random.split(jax.random.key(seed), 5)
    obj = centred(streams_of[0], (2, NY, NX), 0.7, 4.2, ((1, 8), (2, 16)), jnp.float32)
    probe = centred(streams_of[1], (2, M, M), 0.7, 4.2, (), jnp.float32)
    amplitudes = jnp.clip(jnp.exp(math.log(4.0) - 4.3859405 * jax.random.uniform(streams_of[2], (PATTERNS, M, M), jnp.float32) ** levels(streams_of[2], (PATTERNS, M, M), ((0, 128),), -0.2, 0.2)), 0.049804688, 4.0).astype(jnp.bfloat16)
    positions = draw_positions(jax.random.fold_in(streams_of[4], 71), 0)
    return {"obj": obj, "probe": probe, "amplitudes": amplitudes, "positions": positions}


amplitude_floor = 0.1
object_regular = 0.5
probe_regular = 1.0

def reference(obj, probe, amplitudes, positions):
    order = probe.shape[1]
    listed = jnp.arange(positions.shape[0], dtype=jnp.int32)
    obj_re, obj_im = (obj[0], obj[1])
    probe_re, probe_im = (probe[0], probe[1])
    for sweep in range(ITERS):
        probe_c = lax.complex(probe_re, probe_im)
        obj_c = lax.complex(obj_re, obj_im)
        power = probe_re * probe_re + probe_im * probe_im

        def visit(carry, index):
            gathered, numer = carry
            spot = positions[index].astype(jnp.int32)
            window = lax.dynamic_slice(obj_c, (spot[0], spot[1]), (order, order))
            exit_wave = probe_c * window
            far = jnp.fft.fft2(exit_wave, norm='ortho')
            factor = amplitudes[index].astype(obj.dtype) / jnp.sqrt(far.real * far.real + far.imag * far.imag + amplitude_floor)
            revised = jnp.fft.ifft2(far * factor, norm='ortho')
            change = revised - exit_wave
            obj_term = jnp.conj(probe_c) * change
            piece = jnp.stack([obj_term.real, obj_term.imag, power])
            start = (jnp.int32(0), spot[0], spot[1])
            block = lax.dynamic_slice(gathered, start, (3, order, order))
            gathered = lax.dynamic_update_slice(gathered, block + piece, start)
            probe_term = jnp.conj(window) * change
            numer = numer + jnp.stack([probe_term.real, probe_term.imag, window.real * window.real + window.imag * window.imag])
            return ((gathered, numer), None)
        start_sums = (jnp.zeros((3,) + obj_re.shape, obj.dtype), jnp.zeros((3, order, order), obj.dtype))
        (gathered, numer), unused = lax.scan(visit, start_sums, listed)
        new_re = obj_re + gathered[0] / (gathered[2] + object_regular)
        new_im = obj_im + gathered[1] / (gathered[2] + object_regular)
        probe_re = probe_re + numer[0] / (numer[2] + probe_regular)
        probe_im = probe_im + numer[1] / (numer[2] + probe_regular)
        obj_re, obj_im = (new_re, new_im)
    return (jnp.stack([obj_re, obj_im]), jnp.stack([probe_re, probe_im]))
```

```python
import functools

import jax
import jax.numpy as jnp
import numpy as np
from jax import lax
from jax.experimental import pallas as pl
from jax.experimental.pallas import tpu as pltpu
from jax.sharding import PartitionSpec as P

ITERS = 2
amplitude_floor = 0.1
object_regular = 0.5
probe_regular = 1.0

N = 256
H = 128
STRIP = 32


def real_tables():
    n = np.arange(H)
    out = []
    for odd in (0, 1):
        phase = (n[:, None] * (2 * n[None, :] + odd)) % N
        angle = phase * (2 * np.pi / N)
        re, im = np.cos(angle) / 16.0, -np.sin(angle) / 16.0
        full = np.block([[re, im], [-im, re]]).astype(np.float32)
        out += [full, full.T]
    full = jnp.asarray(np.stack(out))
    high = full.astype(jnp.bfloat16)
    low = (full - high.astype(jnp.float32)).astype(jnp.bfloat16)
    return high, low


def order_tables():
    order = np.concatenate([np.arange(0, N, 2), np.arange(1, N, 2)])
    sel = np.zeros((N, N), np.float32)
    sel[np.arange(N), order] = 1.0
    return jnp.asarray(np.stack([sel, sel.T])).astype(jnp.bfloat16)


def split(x):
    high = x.astype(jnp.bfloat16)
    low = (x - high.astype(jnp.float32)).astype(jnp.bfloat16)
    return high, low


def mm(a, b):
    return jnp.dot(a, b, preferred_element_type=jnp.float32)


def pattern_kernel(
    pos_ref,
    place_ref,
    own_ref,
    right_ref,
    below_ref,
    diag_ref,
    probe_ref,
    amps_ref,
    th_ref,
    tl_ref,
    sel_ref,
    sums_ref,
    part_ref,
    ext,
    raw,
    amp,
    win,
    psi,
    ah,
    al,
    ye,
    yo,
    load_sem,
    amp_sem,
):
    band = place_ref[0]
    my_col = place_ref[1]
    loads = []
    for k, (src, r, c) in enumerate(
        ((own_ref, 0, 0), (right_ref, 0, N), (below_ref, N, 0), (diag_ref, N, N))
    ):
        copy = pltpu.make_async_copy(
            src, ext.at[:, pl.ds(r, N), pl.ds(c, N)], load_sem.at[k]
        )
        copy.start()
        loads.append(copy)
    for r in range(0, 2 * N, STRIP):
        for q in range(2):
            sums_ref[q, pl.ds(r, STRIP), :] = jnp.zeros((STRIP, 2 * N), jnp.float32)
    part_ref[...] = jnp.zeros_like(part_ref)
    for copy in loads:
        copy.wait()

    lane = lax.broadcasted_iota(jnp.int32, (STRIP, H), 1)

    def process(j, top, left):
        fetch = pltpu.make_async_copy(amps_ref.at[j], raw, amp_sem)
        fetch.start()
        r8 = pl.multiple_of((top // 8) * 8, 8)
        dr = top - r8
        c128 = pl.multiple_of((left // H) * H, H)
        dc = left - c128

        def cut(s, _):
            r0 = pl.multiple_of(s * STRIP, STRIP)
            w = []
            for q in range(2):
                block = ext[q, pl.ds(r8 + r0, STRIP + 8), pl.ds(c128, 3 * H)]
                block = pltpu.roll(block, lax.rem(STRIP + 8 - dr, STRIP + 8), 0)[:STRIP]
                turned = [
                    pltpu.roll(block[:, k * H : (k + 1) * H], lax.rem(H - dc, H), 1)
                    for k in range(3)
                ]
                keep = lane < H - dc
                w.append(
                    [
                        jnp.where(keep, turned[0], turned[1]),
                        jnp.where(keep, turned[1], turned[2]),
                    ]
                )
            rows = pl.ds(r0, STRIP)
            x = []
            for k in range(2):
                cols = pl.ds(k * H, H)
                wr, wi = w[0][k], w[1][k]
                win[0, rows, cols] = wr
                win[1, rows, cols] = wi
                pr, pi = probe_ref[0, k, rows, :], probe_ref[1, k, rows, :]
                er = pr * wr - pi * wi
                ei = pr * wi + pi * wr
                psi[0, rows, cols] = er
                psi[1, rows, cols] = ei
                x.append((er, ei))
            for k, z in enumerate(
                (
                    x[0][0] + x[1][0],
                    x[0][1] + x[1][1],
                    x[0][0] - x[1][0],
                    x[0][1] - x[1][1],
                )
            ):
                high, low = split(z)
                ah[k // 2, rows, pl.ds((k % 2) * H, H)] = high
                al[k // 2, rows, pl.ds((k % 2) * H, H)] = low
            return 0

        lax.fori_loop(0, N // STRIP, cut, 0)

        def right_apply(t):
            for k, out in ((0, ye), (1, yo)):
                th, tl = th_ref[2 * k + t], tl_ref[2 * k + t]
                out[...] = mm(ah[k], th) + mm(al[k], th) + mm(ah[k], tl)

        def left_apply(t):
            for k, out in ((0, ye), (1, yo)):
                th, tl = th_ref[2 * k + t], tl_ref[2 * k + t]
                out[...] = mm(th, ah[k]) + mm(th, al[k]) + mm(tl, ah[k])

        def put(k, rows, cols, z):
            high, low = split(z)
            ah[k, rows, cols] = high
            al[k, rows, cols] = low

        right_apply(0)

        def rows_forward(s, _):
            r0 = pl.multiple_of(s * STRIP, STRIP)
            up, down = pl.ds(r0, STRIP), pl.ds(r0 + H, STRIP)
            for k, src in ((0, ye), (1, yo)):
                cols = pl.ds(k * H, H)
                for q in range(2):
                    part = pl.ds(q * H, H)
                    a, b = src[up, part], src[down, part]
                    dest = up if q == 0 else down
                    put(0, dest, cols, a + b)
                    put(1, dest, cols, a - b)
            return 0

        lax.fori_loop(0, H // STRIP, rows_forward, 0)
        left_apply(1)
        fetch.wait()
        amp[...] = mm(mm(sel_ref[0], raw[...]).astype(jnp.bfloat16), sel_ref[1])

        def modulus(s, _):
            r0 = pl.multiple_of(s * STRIP, STRIP)
            up, down = pl.ds(r0, STRIP), pl.ds(r0 + H, STRIP)
            for k, src in ((0, ye), (1, yo)):
                re, im = src[up, :], src[down, :]
                m = amp[pl.ds(r0 + k * H, STRIP), :]
                f = m * lax.rsqrt(re * re + im * im + amplitude_floor)
                put(k, up, slice(None), re * f)
                put(k, down, slice(None), im * f)
            return 0

        lax.fori_loop(0, H // STRIP, modulus, 0)
        left_apply(0)

        def rows_back(s, _):
            r0 = pl.multiple_of(s * STRIP, STRIP)
            up, down = pl.ds(r0, STRIP), pl.ds(r0 + H, STRIP)
            for q, src_rows in ((0, up), (1, down)):
                part = pl.ds(q * H, H)
                e, o = ye[src_rows, :], yo[src_rows, :]
                for dest, z in ((up, e + o), (down, e - o)):
                    put(0, dest, part, z[:, :H])
                    put(1, dest, part, z[:, H:])
            return 0

        lax.fori_loop(0, H // STRIP, rows_back, 0)
        right_apply(1)

        def finish(s, _):
            r0 = pl.multiple_of(s * STRIP, STRIP)
            rows = pl.ds(r0, STRIP)
            e_re, e_im = ye[rows, :H], ye[rows, H:]
            o_re, o_im = yo[rows, :H], yo[rows, H:]
            term = [[], []]
            for k in range(2):
                cols = pl.ds(k * H, H)
                br = e_re + o_re if k == 0 else e_re - o_re
                bi = e_im + o_im if k == 0 else e_im - o_im
                cr = br - psi[0, rows, cols]
                ci = bi - psi[1, rows, cols]
                pr, pi = probe_ref[0, k, rows, :], probe_ref[1, k, rows, :]
                wr, wi = win[0, rows, cols], win[1, rows, cols]
                term[0].append(pr * cr + pi * ci)
                term[1].append(pr * ci - pi * cr)
                part_ref[0, k, rows, :] += wr * cr + wi * ci
                part_ref[1, k, rows, :] += wr * ci - wi * cr
                part_ref[2, k, rows, :] += wr * wr + wi * wi
            for q in range(2):
                deposit(sums_ref.at[q], r8 + r0, c128, dr, dc, lane, term[q])
            return 0

        lax.fori_loop(0, N // STRIP, finish, 0)

    def visit(i, _):
        j = band * 64 + i
        y, x = pos_ref[2 * j], pos_ref[2 * j + 1]

        @pl.when(x // N == my_col)
        def _():
            process(i, y - band * N, x - my_col * N)

        return 0

    lax.fori_loop(0, 64, visit, 0)


def deposit(sums, row, col, dr, dc, lane, halves):
    a, b = (pltpu.roll(z, dc, 1) for z in halves)
    hold = lane < dc
    zero = jnp.zeros_like(a)
    wide = jnp.concatenate(
        [jnp.where(hold, zero, a), jnp.where(hold, a, b), jnp.where(hold, b, zero)],
        axis=1,
    )
    tall = jnp.concatenate([wide, jnp.zeros((8, 3 * H), jnp.float32)], axis=0)
    tall = pltpu.roll(tall, dr, 0)
    spot = (pl.ds(pl.multiple_of(row, 8), STRIP + 8), pl.ds(col, 3 * H))
    sums[spot] = sums[spot] + tall


def weights_kernel(pos_ref, place_ref, probe_ref, out_ref, total):
    band = place_ref[0]
    my_col = place_ref[1]
    lane = lax.broadcasted_iota(jnp.int32, (STRIP, H), 1)
    for r in range(0, 3 * N, STRIP):
        total[pl.ds(r, STRIP), :] = jnp.zeros((STRIP, 3 * N), jnp.float32)

    def visit(j, _):
        y, x = pos_ref[2 * j], pos_ref[2 * j + 1]
        top = y - band * N + N
        left = x - my_col * N + N

        @pl.when((top > 0) & (left > 0) & (top < 2 * N) & (left < 2 * N))
        def _():
            r8 = (top // 8) * 8
            c128 = pl.multiple_of((left // H) * H, H)

            def strip(s, _):
                rows = pl.ds(pl.multiple_of(s * STRIP, STRIP), STRIP)
                halves = []
                for k in range(2):
                    cols = pl.ds(k * H, H)
                    pr, pi = probe_ref[0, k, rows, :], probe_ref[1, k, rows, :]
                    halves.append(pr * pr + pi * pi)
                deposit(
                    total, r8 + s * STRIP, c128, top - r8, left - c128, lane, halves
                )
                return 0

            lax.fori_loop(0, N // STRIP, strip, 0)

        return 0

    first = jnp.maximum(band - 1, 0) * 64
    lax.fori_loop(first, (band + 1) * 64, visit, 0)
    out_ref[...] = total[N : 2 * N, N : 2 * N]


SMEM = pl.BlockSpec(memory_space=pltpu.SMEM)
VMEM = pl.BlockSpec(memory_space=pltpu.VMEM)
ANY = pl.BlockSpec(memory_space=pl.ANY)


def run_patterns(pos, place, tiles, probe, gathered, high, low, sel):
    f32, bf16 = jnp.float32, jnp.bfloat16
    return pl.pallas_call(
        pattern_kernel,
        out_shape=(
            jax.ShapeDtypeStruct((2, 2 * N, 2 * N), f32),
            jax.ShapeDtypeStruct((3, 2, N, H), f32),
        ),
        in_specs=[SMEM, SMEM, ANY, ANY, ANY, ANY, VMEM, ANY, VMEM, VMEM, VMEM],
        out_specs=(VMEM, VMEM),
        scratch_shapes=[
            pltpu.VMEM((2, 2 * N, 2 * N), f32),
            pltpu.VMEM((N, N), bf16),
            pltpu.VMEM((N, N), f32),
            pltpu.VMEM((2, N, N), f32),
            pltpu.VMEM((2, N, N), f32),
            pltpu.VMEM((2, N, N), bf16),
            pltpu.VMEM((2, N, N), bf16),
            pltpu.VMEM((N, N), f32),
            pltpu.VMEM((N, N), f32),
            pltpu.SemaphoreType.DMA((4,)),
            pltpu.SemaphoreType.DMA,
        ],
        compiler_params=pltpu.CompilerParams(vmem_limit_bytes=40 * 2**20),
        name="patterns",
    )(pos, place, *tiles, probe, gathered, high, low, sel)


def run_weights(pos, place, probe):
    return pl.pallas_call(
        weights_kernel,
        out_shape=jax.ShapeDtypeStruct((N, N), jnp.float32),
        in_specs=[SMEM, SMEM, VMEM],
        out_specs=VMEM,
        scratch_shapes=[pltpu.VMEM((3 * N, 3 * N), jnp.float32)],
        compiler_params=pltpu.CompilerParams(vmem_limit_bytes=16 * 2**20),
        name="weights",
    )(pos, place, probe)


MESH = pl.DeviceIdType.MESH


def probe_kernel(
    part_ref,
    old_ref,
    out_ref,
    pair,
    half,
    from_x,
    quarter,
    from_y,
    small,
    from_z,
    send_sem,
    recv_sem,
):
    row, col = lax.axis_index("row"), lax.axis_index("col")
    z, y_hi = row // 2, row % 2
    x, y_lo, core = col // 4, (col // 2) % 2, col % 2
    y = y_hi * 2 + y_lo

    def device(z, y, x, core):
        return (z * 2 + y // 2, x * 4 + (y % 2) * 2 + core)

    twin = device(z, y, x, 1 - core)
    on_x = [device(z, y, (x + d) % 4, core) for d in (1, 2, 3)]
    on_y = [device(z, (y + d) % 4, x, core) for d in (1, 2, 3)]
    on_z = [device((z + d) % 4, y, x, core) for d in (1, 2, 3)]
    barrier = pltpu.get_barrier_semaphore()
    for peer in (twin, *on_x, *on_y, *on_z):
        pl.semaphore_signal(barrier, inc=1, device_id=peer, device_id_type=MESH)
    pl.semaphore_wait(barrier, 10)

    count = [0]

    def send(src, dst, peer):
        k = count[0]
        count[0] += 1
        copy = pltpu.make_async_remote_copy(
            src_ref=src,
            dst_ref=dst,
            send_sem=send_sem.at[k],
            recv_sem=recv_sem.at[k],
            device_id=peer,
            device_id_type=MESH,
        )
        copy.start()
        return copy

    def finish(copies):
        for copy in copies:
            copy.wait()

    finish([send(part_ref.at[:, 1 - core], pair, twin)])
    for q in range(3):
        half[q] = part_ref[q, core] + pair[q]
    finish(
        [
            send(
                half.at[:, pl.ds(pl.multiple_of((x + d) % 4 * 64, 64), 64), :],
                from_x.at[d - 1],
                on_x[d - 1],
            )
            for d in (1, 2, 3)
        ]
    )
    mine = pl.ds(pl.multiple_of(x * 64, 64), 64)
    quarter[...] = (half[:, mine, :] + from_x[0]) + (from_x[1] + from_x[2])
    finish(
        [
            send(
                quarter.at[:, pl.ds(pl.multiple_of((y + d) % 4 * 16, 16), 16), :],
                from_y.at[d - 1],
                on_y[d - 1],
            )
            for d in (1, 2, 3)
        ]
    )
    mine = pl.ds(pl.multiple_of(y * 16, 16), 16)
    small[...] = (quarter[:, mine, :] + from_y[0]) + (from_y[1] + from_y[2])
    copies = [send(small, from_z.at[z], peer) for peer in on_z]
    from_z[z] = small[...]
    finish(copies)
    total = (from_z[0] + from_z[1]) + (from_z[2] + from_z[3])
    rows = pl.ds(pl.multiple_of(x * 64 + y * 16, 16), 16)
    for q in range(2):
        out_ref[q, core, rows, :] = old_ref[q, core, rows, :] + total[q] / (
            total[2] + probe_regular
        )
    piece = out_ref.at[:, core, rows, :]
    finish([send(piece, piece, peer) for peer in on_y])
    piece = out_ref.at[:, core, pl.ds(pl.multiple_of(x * 64, 64), 64), :]
    finish([send(piece, piece, peer) for peer in on_x])
    piece = out_ref.at[:, core]
    finish([send(piece, piece, twin)])


def run_probe(partials, probe):
    f32 = jnp.float32
    return pl.pallas_call(
        probe_kernel,
        out_shape=jax.ShapeDtypeStruct((2, 2, N, H), f32),
        in_specs=[VMEM, VMEM],
        out_specs=VMEM,
        scratch_shapes=[
            pltpu.VMEM((3, N, H), f32),
            pltpu.VMEM((3, N, H), f32),
            pltpu.VMEM((3, 3, 64, H), f32),
            pltpu.VMEM((3, 64, H), f32),
            pltpu.VMEM((3, 3, 16, H), f32),
            pltpu.VMEM((3, 16, H), f32),
            pltpu.VMEM((4, 3, 16, H), f32),
            pltpu.SemaphoreType.DMA((17,)),
            pltpu.SemaphoreType.DMA((17,)),
        ],
        compiler_params=pltpu.CompilerParams(
            collective_id=1, has_side_effects=True, vmem_limit_bytes=16 * 2**20
        ),
        name="probe_sum",
    )(partials, probe)


def shifts(rows, cols, down):
    near = [(r, r + 1) for r in range(rows - 1)]
    side = [(c, c + 1) for c in range(cols - 1)]
    both = [
        (r * cols + c, (r + 1) * cols + c + 1)
        for r in range(rows - 1)
        for c in range(cols - 1)
    ]
    if not down:
        near, side, both = ([(b, a) for a, b in z] for z in (near, side, both))
    return near, side, both


def neighbours(tile, rows, cols):
    near, side, both = shifts(rows, cols, False)
    return (
        tile,
        lax.ppermute(tile, "col", side),
        lax.ppermute(tile, "row", near),
        lax.ppermute(tile, ("row", "col"), both),
    )


def local(rows, cols, obj, probe, amplitudes, positions):
    place = jnp.stack([lax.axis_index("row"), lax.axis_index("col")]).astype(jnp.int32)
    pos = positions.reshape(-1)
    high, low = real_tables()
    sel = order_tables()
    gathered = lax.all_gather(amplitudes, "col", tiled=True)
    near, side, both = shifts(rows, cols, True)
    tile = obj
    illum = jnp.stack([probe[:, :, :H], probe[:, :, H:]], axis=1)
    for sweep in range(ITERS):
        tiles = neighbours(tile, rows, cols)
        sums, partials = run_patterns(pos, place, tiles, illum, gathered, high, low, sel)
        from_left = lax.ppermute(sums[:, :N, N:], "col", side)
        from_above = lax.ppermute(sums[:, N:, :N], "row", near)
        from_both = lax.ppermute(sums[:, N:, N:], ("row", "col"), both)
        weights = run_weights(pos, place, illum)
        grad = sums[:, :N, :N] + from_left + from_above + from_both
        tile = tile + grad / (weights + object_regular)[None]
        illum = run_probe(partials, illum)
    return tile, jnp.concatenate([illum[:, 0], illum[:, 1]], axis=2)


def solution(mesh):
    rows, cols = mesh.shape["row"], mesh.shape["col"]
    placed = (P(None, "row", "col"), P(), P(("row", "col"), None, None), P())
    return jax.shard_map(
        functools.partial(local, rows, cols),
        mesh=mesh,
        in_specs=placed,
        out_specs=(P(None, "row", "col"), P()),
        check_vma=False,
    )
```

```python
import functools

import jax
import jax.numpy as jnp
import numpy as np
from jax import lax
from jax.experimental import pallas as pl
from jax.experimental.pallas import tpu as pltpu
from jax.sharding import PartitionSpec as P

ITERS = 2
amplitude_floor = 0.1
object_regular = 0.5
probe_regular = 1.0

N = 256
H = 128
STRIP = 32


def real_tables():
    n = np.arange(H)
    out = []
    for odd in (0, 1):
        phase = (n[:, None] * (2 * n[None, :] + odd)) % N
        angle = phase * (2 * np.pi / N)
        re, im = np.cos(angle) / 16.0, -np.sin(angle) / 16.0
        full = np.block([[re, im], [-im, re]]).astype(np.float32)
        out += [full, full.T]
    full = jnp.asarray(np.stack(out))
    high = full.astype(jnp.bfloat16)
    low = (full - high.astype(jnp.float32)).astype(jnp.bfloat16)
    return high, low


def order_tables():
    order = np.concatenate([np.arange(0, N, 2), np.arange(1, N, 2)])
    sel = np.zeros((N, N), np.float32)
    sel[np.arange(N), order] = 1.0
    return jnp.asarray(np.stack([sel, sel.T])).astype(jnp.bfloat16)


def split(x):
    high = x.astype(jnp.bfloat16)
    low = (x - high.astype(jnp.float32)).astype(jnp.bfloat16)
    return high, low


def mm(a, b):
    return jnp.dot(a, b, preferred_element_type=jnp.float32)


def pattern_kernel(
    pos_ref,
    place_ref,
    ext,
    probe_ref,
    amps_ref,
    th_ref,
    tl_ref,
    sel_ref,
    sums_ref,
    part_ref,
    raw,
    amp,
    win,
    psi,
    ah,
    al,
    ye,
    yo,
    amp_sem,
):
    band = place_ref[0]
    my_col = place_ref[1]
    for r in range(0, 2 * N, STRIP):
        for q in range(2):
            sums_ref[q, pl.ds(r, STRIP), :] = jnp.zeros((STRIP, 2 * N), jnp.float32)
    part_ref[...] = jnp.zeros_like(part_ref)

    lane = lax.broadcasted_iota(jnp.int32, (STRIP, H), 1)

    def process(j, top, left):
        fetch = pltpu.make_async_copy(amps_ref.at[j], raw, amp_sem)
        fetch.start()
        r8 = pl.multiple_of((top // 8) * 8, 8)
        dr = top - r8
        c128 = pl.multiple_of((left // H) * H, H)
        dc = left - c128

        def cut(s, _):
            r0 = pl.multiple_of(s * STRIP, STRIP)
            w = []
            for q in range(2):
                block = ext[q, pl.ds(r8 + r0, STRIP + 8), pl.ds(c128, 3 * H)]
                block = pltpu.roll(block, lax.rem(STRIP + 8 - dr, STRIP + 8), 0)[:STRIP]
                turned = [
                    pltpu.roll(block[:, k * H : (k + 1) * H], lax.rem(H - dc, H), 1)
                    for k in range(3)
                ]
                keep = lane < H - dc
                w.append(
                    [
                        jnp.where(keep, turned[0], turned[1]),
                        jnp.where(keep, turned[1], turned[2]),
                    ]
                )
            rows = pl.ds(r0, STRIP)
            x = []
            for k in range(2):
                cols = pl.ds(k * H, H)
                wr, wi = w[0][k], w[1][k]
                win[0, rows, cols] = wr
                win[1, rows, cols] = wi
                pr, pi = probe_ref[0, k, rows, :], probe_ref[1, k, rows, :]
                er = pr * wr - pi * wi
                ei = pr * wi + pi * wr
                psi[0, rows, cols] = er
                psi[1, rows, cols] = ei
                x.append((er, ei))
            for k, z in enumerate(
                (
                    x[0][0] + x[1][0],
                    x[0][1] + x[1][1],
                    x[0][0] - x[1][0],
                    x[0][1] - x[1][1],
                )
            ):
                high, low = split(z)
                ah[k // 2, rows, pl.ds((k % 2) * H, H)] = high
                al[k // 2, rows, pl.ds((k % 2) * H, H)] = low
            return 0

        lax.fori_loop(0, N // STRIP, cut, 0, unroll=8)

        def right_apply(t):
            for k, out in ((0, ye), (1, yo)):
                th, tl = th_ref[2 * k + t], tl_ref[2 * k + t]
                out[...] = mm(ah[k], th) + mm(al[k], th) + mm(ah[k], tl)

        def left_apply(t):
            for k, out in ((0, ye), (1, yo)):
                th, tl = th_ref[2 * k + t], tl_ref[2 * k + t]
                out[...] = mm(th, ah[k]) + mm(th, al[k]) + mm(tl, ah[k])

        def put(k, rows, cols, z):
            high, low = split(z)
            ah[k, rows, cols] = high
            al[k, rows, cols] = low

        right_apply(0)

        def rows_forward(s, _):
            r0 = pl.multiple_of(s * STRIP, STRIP)
            up, down = pl.ds(r0, STRIP), pl.ds(r0 + H, STRIP)
            for k, src in ((0, ye), (1, yo)):
                cols = pl.ds(k * H, H)
                for q in range(2):
                    part = pl.ds(q * H, H)
                    a, b = src[up, part], src[down, part]
                    dest = up if q == 0 else down
                    put(0, dest, cols, a + b)
                    put(1, dest, cols, a - b)
            return 0

        lax.fori_loop(0, H // STRIP, rows_forward, 0, unroll=4)
        left_apply(1)
        fetch.wait()
        amp[...] = mm(mm(sel_ref[0], raw[...]).astype(jnp.bfloat16), sel_ref[1])

        def modulus(s, _):
            r0 = pl.multiple_of(s * STRIP, STRIP)
            up, down = pl.ds(r0, STRIP), pl.ds(r0 + H, STRIP)
            for k, src in ((0, ye), (1, yo)):
                re, im = src[up, :], src[down, :]
                m = amp[pl.ds(r0 + k * H, STRIP), :]
                f = m * lax.rsqrt(re * re + im * im + amplitude_floor)
                put(k, up, slice(None), re * f)
                put(k, down, slice(None), im * f)
            return 0

        lax.fori_loop(0, H // STRIP, modulus, 0, unroll=4)
        left_apply(0)

        def rows_back(s, _):
            r0 = pl.multiple_of(s * STRIP, STRIP)
            up, down = pl.ds(r0, STRIP), pl.ds(r0 + H, STRIP)
            for q, src_rows in ((0, up), (1, down)):
                part = pl.ds(q * H, H)
                e, o = ye[src_rows, :], yo[src_rows, :]
                for dest, z in ((up, e + o), (down, e - o)):
                    put(0, dest, part, z[:, :H])
                    put(1, dest, part, z[:, H:])
            return 0

        lax.fori_loop(0, H // STRIP, rows_back, 0, unroll=4)
        right_apply(1)

        def finish(s, _):
            r0 = pl.multiple_of(s * STRIP, STRIP)
            rows = pl.ds(r0, STRIP)
            e_re, e_im = ye[rows, :H], ye[rows, H:]
            o_re, o_im = yo[rows, :H], yo[rows, H:]
            term = [[], []]
            for k in range(2):
                cols = pl.ds(k * H, H)
                br = e_re + o_re if k == 0 else e_re - o_re
                bi = e_im + o_im if k == 0 else e_im - o_im
                cr = br - psi[0, rows, cols]
                ci = bi - psi[1, rows, cols]
                pr, pi = probe_ref[0, k, rows, :], probe_ref[1, k, rows, :]
                wr, wi = win[0, rows, cols], win[1, rows, cols]
                term[0].append(pr * cr + pi * ci)
                term[1].append(pr * ci - pi * cr)
                part_ref[0, k, rows, :] += wr * cr + wi * ci
                part_ref[1, k, rows, :] += wr * ci - wi * cr
                part_ref[2, k, rows, :] += wr * wr + wi * wi
            for q in range(2):
                deposit(sums_ref.at[q], r8 + r0, c128, dr, dc, lane, term[q])
            return 0

        lax.fori_loop(0, N // STRIP, finish, 0, unroll=8)

    def visit(i, _):
        j = band * 64 + i
        y, x = pos_ref[2 * j], pos_ref[2 * j + 1]

        @pl.when(x // N == my_col)
        def _():
            process(i, y - band * N, x - my_col * N)

        return 0

    lax.fori_loop(0, 64, visit, 0)


def deposit(sums, row, col, dr, dc, lane, halves):
    a, b = (pltpu.roll(z, dc, 1) for z in halves)
    hold = lane < dc
    zero = jnp.zeros_like(a)
    wide = jnp.concatenate(
        [jnp.where(hold, zero, a), jnp.where(hold, a, b), jnp.where(hold, b, zero)],
        axis=1,
    )
    tall = jnp.concatenate([wide, jnp.zeros((8, 3 * H), jnp.float32)], axis=0)
    tall = pltpu.roll(tall, dr, 0)
    spot = (pl.ds(pl.multiple_of(row, 8), STRIP + 8), pl.ds(col, 3 * H))
    sums[spot] = sums[spot] + tall


def weights_kernel(pos_ref, place_ref, probe_ref, out_ref, total, power):
    band = place_ref[0]
    my_col = place_ref[1]
    lane = lax.broadcasted_iota(jnp.int32, (STRIP, H), 1)
    power[...] = probe_ref[0] * probe_ref[0] + probe_ref[1] * probe_ref[1]
    for r in range(0, 3 * N, STRIP):
        total[pl.ds(r, STRIP), :] = jnp.zeros((STRIP, 3 * N), jnp.float32)

    def visit(j, _):
        y, x = pos_ref[2 * j], pos_ref[2 * j + 1]
        top = y - band * N + N
        left = x - my_col * N + N

        @pl.when((top > 0) & (left > 0) & (top < 2 * N) & (left < 2 * N))
        def _():
            r8 = (top // 8) * 8
            c128 = pl.multiple_of((left // H) * H, H)

            for s in range(N // STRIP):
                low = top + s * STRIP

                @pl.when((low + STRIP > N) & (low < 2 * N))
                def _(s=s):
                    rows = pl.ds(s * STRIP, STRIP)
                    halves = [power[k, rows, :] for k in range(2)]
                    deposit(
                        total, r8 + s * STRIP, c128, top - r8, left - c128, lane, halves
                    )

        return 0

    first = jnp.maximum(band - 1, 0) * 64
    lax.fori_loop(first, (band + 1) * 64, visit, 0)
    out_ref[...] = total[N : 2 * N, N : 2 * N]


SMEM = pl.BlockSpec(memory_space=pltpu.SMEM)
VMEM = pl.BlockSpec(memory_space=pltpu.VMEM)
ANY = pl.BlockSpec(memory_space=pl.ANY)


def run_patterns(pos, place, ext, probe, gathered, high, low, sel):
    f32, bf16 = jnp.float32, jnp.bfloat16
    return pl.pallas_call(
        pattern_kernel,
        out_shape=(
            jax.ShapeDtypeStruct((2, 2 * N, 2 * N), f32),
            jax.ShapeDtypeStruct((3, 2, N, H), f32),
        ),
        in_specs=[SMEM, SMEM, VMEM, VMEM, ANY, VMEM, VMEM, VMEM],
        out_specs=(VMEM, VMEM),
        scratch_shapes=[
            pltpu.VMEM((N, N), bf16),
            pltpu.VMEM((N, N), f32),
            pltpu.VMEM((2, N, N), f32),
            pltpu.VMEM((2, N, N), f32),
            pltpu.VMEM((2, N, N), bf16),
            pltpu.VMEM((2, N, N), bf16),
            pltpu.VMEM((N, N), f32),
            pltpu.VMEM((N, N), f32),
            pltpu.SemaphoreType.DMA,
        ],
        compiler_params=pltpu.CompilerParams(vmem_limit_bytes=40 * 2**20),
        name="patterns",
    )(pos, place, ext, probe, gathered, high, low, sel)


def run_weights(pos, place, probe):
    return pl.pallas_call(
        weights_kernel,
        out_shape=jax.ShapeDtypeStruct((N, N), jnp.float32),
        in_specs=[SMEM, SMEM, VMEM],
        out_specs=VMEM,
        scratch_shapes=[
            pltpu.VMEM((3 * N, 3 * N), jnp.float32),
            pltpu.VMEM((2, N, H), jnp.float32),
        ],
        compiler_params=pltpu.CompilerParams(vmem_limit_bytes=16 * 2**20),
        name="weights",
    )(pos, place, probe)


MESH = pl.DeviceIdType.MESH


def whereabouts():
    row, col = lax.axis_index("row"), lax.axis_index("col")
    z, y = row // 2, (row % 2) * 2 + (col // 2) % 2
    x, core = col // 4, col % 2

    def device(z, y, x, core):
        return (z * 2 + y // 2, x * 4 + (y % 2) * 2 + core)

    return row, col, z, y, x, core, device


def greet(peers):
    barrier = pltpu.get_barrier_semaphore()
    for peer in peers:
        pl.semaphore_signal(barrier, inc=1, device_id=peer, device_id_type=MESH)
    pl.semaphore_wait(barrier, len(peers))


class Copies:
    def __init__(self, send_sem, recv_sem):
        self.send_sem, self.recv_sem, self.made = send_sem, recv_sem, []

    def make(self, src, dst, peer, k=None):
        if k is None:
            k = len(self.made)
            self.made.append(None)
        copy = pltpu.make_async_remote_copy(
            src_ref=src,
            dst_ref=dst,
            send_sem=self.send_sem.at[k],
            recv_sem=self.recv_sem.at[k],
            device_id=peer,
            device_id_type=MESH,
        )
        self.made[k] = copy
        return copy, k

    def send(self, src, dst, peer):
        copy, _ = self.make(src, dst, peer)
        copy.start()
        return copy


def around(row, col):
    left, right = lax.rem(col + 15, 16), lax.rem(col + 1, 16)
    up, down = lax.rem(row + 7, 8), lax.rem(row + 1, 8)
    return left, right, up, down


TOP, END = slice(0, N), slice(N, 2 * N)


class Halo:
    def __init__(self, copies, tile, ext, row, col, core):
        left, right, up, down = around(row, col)
        self.core = core
        self.below = copies.send(tile, ext.at[:, END, TOP], (up, col))
        self.right = copies.send(tile, ext.at[:, TOP, END], (row, left))
        corner = ext.at[:, END, END]
        self.diag, k = copies.make(tile, corner, (up, left))
        self.onward, _ = copies.make(ext.at[:, END, TOP], corner, (row, left), k)

        @pl.when(core == 0)
        def _():
            self.diag.start()

    def pass_on(self):
        self.below.wait_recv()

        @pl.when(self.core == 1)
        def _():
            self.onward.start()

    def finish(self):
        self.below.wait_send()
        self.right.wait()
        self.diag.wait()


def start_kernel(obj_ref, amps_ref, ext_ref, all_ref, send_sem, recv_sem, own_sem):
    row, col, z, y, x, core, device = whereabouts()
    left, right, up, down = around(row, col)
    twin = device(z, y, x, 1 - core)
    beside = device(z, y + 1 - 2 * (y % 2), x, core)
    ahead, behind = device(z, y, (x + 1) % 4, core), device(z, y, (x + 3) % 4, core)
    greet(
        [
            twin,
            beside,
            ahead,
            behind,
            (row, left),
            (row, right),
            (up, col),
            (down, col),
            (up, left),
            (down, right),
        ]
    )
    copies = Copies(send_sem, recv_sem)

    def block(x, ylo, first=0, count=4):
        c = (x % 4) * 4 + ylo * 2 + core
        return all_ref.at[pl.ds(c * 4 + first, count)]

    ylo = y % 2
    mine, other = block(x, ylo), block(x, 1 - ylo)
    to_beside = copies.send(amps_ref, mine, beside)
    to_ahead = copies.send(amps_ref, mine, ahead)
    to_behind = copies.send(amps_ref, mine, behind)
    halo = Halo(copies, obj_ref, ext_ref, row, col, core)
    own = [
        pltpu.make_async_copy(amps_ref, mine, own_sem.at[0]),
        pltpu.make_async_copy(obj_ref, ext_ref.at[:, TOP, TOP], own_sem.at[1]),
    ]
    for copy in own:
        copy.start()
    rest = [copies.send(amps_ref, mine, twin)]
    to_beside.wait_recv()
    ahead_2 = copies.send(other, other, ahead)
    behind_2 = copies.send(other, other, behind)
    rest.append(copies.send(other, other, twin))
    far = []
    for low, high, side in ((to_ahead, to_behind, ylo), (ahead_2, behind_2, 1 - ylo)):
        low.wait_recv()
        part = block(x + 3, side, 0, 2)
        far.append((copies.send(part, part, ahead), block(x + 2, side, 0, 2)))
        whole = block(x + 3, side)
        rest.append(copies.send(whole, whole, twin))
        high.wait_recv()
        part = block(x + 1, side, 2, 2)
        far.append((copies.send(part, part, behind), block(x + 2, side, 2, 2)))
        whole = block(x + 1, side)
        rest.append(copies.send(whole, whole, twin))
        if side is ylo:
            halo.pass_on()
    for copy, part in far:
        copy.wait_recv()
        rest.append(copies.send(part, part, twin))
    for copy in own:
        copy.wait()
    for copy in (to_beside, to_ahead, to_behind, ahead_2, behind_2):
        copy.wait_send()
    for copy, _ in far:
        copy.wait_send()
    for copy in rest:
        copy.wait()
    halo.finish()


def run_start(obj, amplitudes):
    count = 3 + 3 + 1 + 3 + 8 + 4
    return pl.pallas_call(
        start_kernel,
        out_shape=(
            jax.ShapeDtypeStruct((2, 2 * N, 2 * N), jnp.float32),
            jax.ShapeDtypeStruct((64, N, N), jnp.bfloat16),
        ),
        in_specs=[VMEM, ANY],
        out_specs=(VMEM, ANY),
        scratch_shapes=[
            pltpu.SemaphoreType.DMA((count,)),
            pltpu.SemaphoreType.DMA((count,)),
            pltpu.SemaphoreType.DMA((2,)),
        ],
        compiler_params=pltpu.CompilerParams(
            collective_id=1, has_side_effects=True, vmem_limit_bytes=16 * 2**20
        ),
        name="start",
    )(obj, amplitudes)


def exchange_kernel(
    last,
    sums_ref,
    weights_ref,
    ext_ref,
    part_ref,
    old_ref,
    tile_ref,
    out_ref,
    from_left,
    from_above,
    corner,
    low,
    pair,
    half,
    from_x,
    quarter,
    from_y,
    small,
    from_z,
    send_sem,
    recv_sem,
):
    row, col, z, y, x, core, device = whereabouts()
    left, right, up, down = around(row, col)
    twin = device(z, y, x, 1 - core)
    on_x = [device(z, y, (x + d) % 4, core) for d in (1, 2, 3)]
    on_y = [device(z, (y + d) % 4, x, core) for d in (1, 2, 3)]
    on_z = [device((z + d) % 4, y, x, core) for d in (1, 2, 3)]
    greet(
        [
            (row, left),
            (row, right),
            (up, col),
            (down, col),
            (up, left),
            (down, right),
            twin,
            *on_x,
            *on_y,
            *on_z,
        ]
    )
    copies = Copies(send_sem, recv_sem)

    def finish(group):
        for copy in group:
            copy.wait()

    edge = sums_ref.at[:, END, END]
    inside, k = copies.make(edge, corner, twin)
    outside, _ = copies.make(edge, corner, (down, right), k)

    @pl.when(core == 0)
    def _():
        inside.start()

    on_pair = copies.send(part_ref.at[:, 1 - core], pair, twin)
    down_sums, k = copies.make(sums_ref.at[:, END, TOP], from_above, (down, col))
    down_joint, _ = copies.make(low, from_above, (down, col), k)

    @pl.when(core == 0)
    def _():
        down_sums.start()

    @pl.when(core == 1)
    def _():
        outside.start()
        inside.wait_recv()
        low[...] = sums_ref[:, END, TOP] + corner[...]
        down_joint.start()

    to_right = copies.send(sums_ref.at[:, TOP, END], from_left, (row, right))

    on_pair.wait()
    for q in range(3):
        half[q] = part_ref[q, core] + pair[q]
    finish(
        [
            copies.send(
                half.at[:, pl.ds(pl.multiple_of((x + d) % 4 * 64, 64), 64), :],
                from_x.at[d - 1],
                on_x[d - 1],
            )
            for d in (1, 2, 3)
        ]
    )
    mine = pl.ds(pl.multiple_of(x * 64, 64), 64)
    quarter[...] = (half[:, mine, :] + from_x[0]) + (from_x[1] + from_x[2])
    finish(
        [
            copies.send(
                quarter.at[:, pl.ds(pl.multiple_of((y + d) % 4 * 16, 16), 16), :],
                from_y.at[d - 1],
                on_y[d - 1],
            )
            for d in (1, 2, 3)
        ]
    )
    mine = pl.ds(pl.multiple_of(y * 16, 16), 16)
    small[...] = (quarter[:, mine, :] + from_y[0]) + (from_y[1] + from_y[2])
    whole = [copies.send(small, from_z.at[z], peer) for peer in on_z]
    from_z[z] = small[...]

    def object_update():
        to_right.wait()
        down_sums.wait()

        @pl.when(core == 0)
        def _():
            outside.wait_recv()

        inside.wait_send()
        for r in range(0, N, STRIP):
            rows = pl.ds(r, STRIP)
            scale = 1.0 / (weights_ref[rows, :] + object_regular)
            for q in range(2):
                total = sums_ref[q, rows, TOP] + from_left[q, rows, :]
                total = total + from_above[q, rows, :]
                total = total + jnp.where(core == 0, corner[q, rows, :], 0.0)
                tile_ref[q, rows, TOP] = ext_ref[q, rows, TOP] + total * scale

    if not last:
        object_update()
        halo = Halo(copies, tile_ref.at[:, TOP, TOP], tile_ref, row, col, core)
    finish(whole)
    total = (from_z[0] + from_z[1]) + (from_z[2] + from_z[3])
    rows = pl.ds(pl.multiple_of(x * 64 + y * 16, 16), 16)
    for q in range(2):
        out_ref[q, core, rows, :] = old_ref[q, core, rows, :] + total[q] / (
            total[2] + probe_regular
        )
    piece = out_ref.at[:, core, rows, :]
    finish([copies.send(piece, piece, peer) for peer in on_y])
    piece = out_ref.at[:, core, pl.ds(pl.multiple_of(x * 64, 64), 64), :]
    finish([copies.send(piece, piece, peer) for peer in on_x])
    piece = out_ref.at[:, core]
    to_twin = copies.send(piece, piece, twin)
    if last:
        object_update()
    else:
        halo.pass_on()
        halo.finish()
    to_twin.wait()


def run_exchange(last, sums, weights, ext, partials, probe):
    f32 = jnp.float32
    count = 4 + 9 + (0 if last else 3) + 7
    tile = (2, N, N) if last else (2, 2 * N, 2 * N)
    return pl.pallas_call(
        functools.partial(exchange_kernel, last),
        out_shape=(
            jax.ShapeDtypeStruct(tile, f32),
            jax.ShapeDtypeStruct((2, 2, N, H), f32),
        ),
        in_specs=[VMEM] * 5,
        out_specs=(VMEM, VMEM),
        scratch_shapes=[
            pltpu.VMEM((2, N, N), f32),
            pltpu.VMEM((2, N, N), f32),
            pltpu.VMEM((2, N, N), f32),
            pltpu.VMEM((2, N, N), f32),
            pltpu.VMEM((3, N, H), f32),
            pltpu.VMEM((3, N, H), f32),
            pltpu.VMEM((3, 3, 64, H), f32),
            pltpu.VMEM((3, 64, H), f32),
            pltpu.VMEM((3, 3, 16, H), f32),
            pltpu.VMEM((3, 16, H), f32),
            pltpu.VMEM((4, 3, 16, H), f32),
            pltpu.SemaphoreType.DMA((count,)),
            pltpu.SemaphoreType.DMA((count,)),
        ],
        compiler_params=pltpu.CompilerParams(
            collective_id=3 if last else 2,
            has_side_effects=True,
            vmem_limit_bytes=32 * 2**20,
        ),
        name="finish" if last else "exchange",
    )(sums, weights, ext, partials, probe)


def local(obj, probe, amplitudes, positions):
    place = jnp.stack([lax.axis_index("row"), lax.axis_index("col")]).astype(jnp.int32)
    pos = positions.reshape(-1)
    high, low = real_tables()
    sel = order_tables()
    illum = jnp.stack([probe[:, :, :H], probe[:, :, H:]], axis=1)
    weights = run_weights(pos, place, illum)
    ext, gathered = run_start(obj, amplitudes)
    for sweep in range(ITERS):
        sums, partials = run_patterns(pos, place, ext, illum, gathered, high, low, sel)
        last = sweep == ITERS - 1
        ext, illum = run_exchange(last, sums, weights, ext, partials, illum)
        if not last:
            weights = run_weights(pos, place, illum)
    return ext, jnp.concatenate([illum[:, 0], illum[:, 1]], axis=2)


def solution(mesh):
    placed = (P(None, "row", "col"), P(), P(("row", "col"), None, None), P())
    return jax.shard_map(
        local,
        mesh=mesh,
        in_specs=placed,
        out_specs=(P(None, "row", "col"), P()),
        check_vma=False,
    )
```

```python
import functools

import jax
import jax.numpy as jnp
import numpy as np
from jax import lax
from jax.experimental import pallas as pl
from jax.experimental.pallas import tpu as pltpu
from jax.sharding import PartitionSpec as P

ITERS = 2
amplitude_floor = 0.1
object_regular = 0.5
probe_regular = 1.0

N = 256
NEAR = 32
FAR = 4096
H = 128
STRIP = 32


def real_tables():
    n = np.arange(H)
    out = []
    for odd in (0, 1):
        phase = (n[:, None] * (2 * n[None, :] + odd)) % N
        angle = phase * (2 * np.pi / N)
        re, im = np.cos(angle) / 16.0, -np.sin(angle) / 16.0
        full = np.block([[re, im], [-im, re]]).astype(np.float32)
        out += [full, full.T]
    full = jnp.asarray(np.stack(out))
    high = full.astype(jnp.bfloat16)
    low = (full - high.astype(jnp.float32)).astype(jnp.bfloat16)
    return high, low


def order_tables():
    order = np.concatenate([np.arange(0, N, 2), np.arange(1, N, 2)])
    sel = np.zeros((N, N), np.float32)
    sel[np.arange(N), order] = 1.0
    return jnp.asarray(np.stack([sel, sel.T])).astype(jnp.bfloat16)


def split(x):
    high = x.astype(jnp.bfloat16)
    low = (x - high.astype(jnp.float32)).astype(jnp.bfloat16)
    return high, low


def mm(a, b):
    return jnp.dot(a, b, preferred_element_type=jnp.float32)


def pattern_kernel(
    first,
    pos_ref,
    place_ref,
    ext,
    probe_ref,
    amps_ref,
    th_ref,
    tl_ref,
    sel_ref,
    sums_ref,
    part_ref,
    near_ref,
    raw,
    amp,
    win,
    psi,
    ah,
    al,
    ye,
    yo,
    amp_sem,
):
    band = place_ref[0]
    my_col = place_ref[1]
    for r in range(0, 2 * N, STRIP):
        for q in range(2):
            sums_ref[q, pl.ds(r, STRIP), :] = jnp.zeros((STRIP, 2 * N), jnp.float32)
    part_ref[...] = jnp.zeros_like(part_ref)

    lane = lax.broadcasted_iota(jnp.int32, (STRIP, H), 1)

    def process(j, top, left):
        fetch = pltpu.make_async_copy(amps_ref.at[j], raw, amp_sem)
        fetch.start()
        r8 = pl.multiple_of((top // 8) * 8, 8)
        dr = top - r8
        c128 = pl.multiple_of((left // H) * H, H)
        dc = left - c128

        def cut(s, _):
            r0 = pl.multiple_of(s * STRIP, STRIP)
            w = []
            for q in range(2):
                block = ext[q, pl.ds(r8 + r0, STRIP + 8), pl.ds(c128, 3 * H)]
                block = pltpu.roll(block, lax.rem(STRIP + 8 - dr, STRIP + 8), 0)[:STRIP]
                turned = [
                    pltpu.roll(block[:, k * H : (k + 1) * H], lax.rem(H - dc, H), 1)
                    for k in range(3)
                ]
                keep = lane < H - dc
                w.append(
                    [
                        jnp.where(keep, turned[0], turned[1]),
                        jnp.where(keep, turned[1], turned[2]),
                    ]
                )
            rows = pl.ds(r0, STRIP)
            x = []
            for k in range(2):
                cols = pl.ds(k * H, H)
                wr, wi = w[0][k], w[1][k]
                win[0, rows, cols] = wr
                win[1, rows, cols] = wi
                pr, pi = probe_ref[0, k, rows, :], probe_ref[1, k, rows, :]
                er = pr * wr - pi * wi
                ei = pr * wi + pi * wr
                psi[0, rows, cols] = er
                psi[1, rows, cols] = ei
                x.append((er, ei))
            for k, z in enumerate(
                (
                    x[0][0] + x[1][0],
                    x[0][1] + x[1][1],
                    x[0][0] - x[1][0],
                    x[0][1] - x[1][1],
                )
            ):
                high, low = split(z)
                ah[k // 2, rows, pl.ds((k % 2) * H, H)] = high
                al[k // 2, rows, pl.ds((k % 2) * H, H)] = low
            return 0

        lax.fori_loop(0, N // STRIP, cut, 0, unroll=8)

        def right_apply(t):
            for k, out in ((0, ye), (1, yo)):
                th, tl = th_ref[2 * k + t], tl_ref[2 * k + t]
                out[...] = mm(ah[k], th) + mm(al[k], th) + mm(ah[k], tl)

        def left_apply(t):
            for k, out in ((0, ye), (1, yo)):
                th, tl = th_ref[2 * k + t], tl_ref[2 * k + t]
                out[...] = mm(th, ah[k]) + mm(th, al[k]) + mm(tl, ah[k])

        def put(k, rows, cols, z):
            high, low = split(z)
            ah[k, rows, cols] = high
            al[k, rows, cols] = low

        right_apply(0)

        def rows_forward(s, _):
            r0 = pl.multiple_of(s * STRIP, STRIP)
            up, down = pl.ds(r0, STRIP), pl.ds(r0 + H, STRIP)
            for k, src in ((0, ye), (1, yo)):
                cols = pl.ds(k * H, H)
                for q in range(2):
                    part = pl.ds(q * H, H)
                    a, b = src[up, part], src[down, part]
                    dest = up if q == 0 else down
                    put(0, dest, cols, a + b)
                    put(1, dest, cols, a - b)
            return 0

        lax.fori_loop(0, H // STRIP, rows_forward, 0, unroll=4)
        left_apply(1)
        fetch.wait()
        amp[...] = mm(mm(sel_ref[0], raw[...]).astype(jnp.bfloat16), sel_ref[1])

        def modulus(s, _):
            r0 = pl.multiple_of(s * STRIP, STRIP)
            up, down = pl.ds(r0, STRIP), pl.ds(r0 + H, STRIP)
            for k, src in ((0, ye), (1, yo)):
                re, im = src[up, :], src[down, :]
                m = amp[pl.ds(r0 + k * H, STRIP), :]
                f = m * lax.rsqrt(re * re + im * im + amplitude_floor)
                put(k, up, slice(None), re * f)
                put(k, down, slice(None), im * f)
            return 0

        lax.fori_loop(0, H // STRIP, modulus, 0, unroll=4)
        left_apply(0)

        def rows_back(s, _):
            r0 = pl.multiple_of(s * STRIP, STRIP)
            up, down = pl.ds(r0, STRIP), pl.ds(r0 + H, STRIP)
            for q, src_rows in ((0, up), (1, down)):
                part = pl.ds(q * H, H)
                e, o = ye[src_rows, :], yo[src_rows, :]
                for dest, z in ((up, e + o), (down, e - o)):
                    put(0, dest, part, z[:, :H])
                    put(1, dest, part, z[:, H:])
            return 0

        lax.fori_loop(0, H // STRIP, rows_back, 0, unroll=4)
        right_apply(1)

        def finish(s, _):
            r0 = pl.multiple_of(s * STRIP, STRIP)
            rows = pl.ds(r0, STRIP)
            e_re, e_im = ye[rows, :H], ye[rows, H:]
            o_re, o_im = yo[rows, :H], yo[rows, H:]
            term = [[], []]
            for k in range(2):
                cols = pl.ds(k * H, H)
                br = e_re + o_re if k == 0 else e_re - o_re
                bi = e_im + o_im if k == 0 else e_im - o_im
                cr = br - psi[0, rows, cols]
                ci = bi - psi[1, rows, cols]
                pr, pi = probe_ref[0, k, rows, :], probe_ref[1, k, rows, :]
                wr, wi = win[0, rows, cols], win[1, rows, cols]
                term[0].append(pr * cr + pi * ci)
                term[1].append(pr * ci - pi * cr)
                part_ref[0, k, rows, :] += wr * cr + wi * ci
                part_ref[1, k, rows, :] += wr * ci - wi * cr
                part_ref[2, k, rows, :] += wr * wr + wi * wi
            for q in range(2):
                deposit(sums_ref.at[q], r8 + r0, c128, dr, dc, lane, term[q])
            return 0

        lax.fori_loop(0, N // STRIP, finish, 0, unroll=8)

    def visit(i, _):
        j = band * 64 + i
        y, x = pos_ref[2 * j], pos_ref[2 * j + 1]

        @pl.when(x // N == my_col)
        def _():
            process(i, y - band * N, x - my_col * N)

        return 0

    lax.fori_loop(0, 64, visit, 0)
    if not first:
        return

    for k in range(2 * NEAR):
        near_ref[k] = FAR

    def note(j, found):
        dy = pos_ref[2 * j] - band * N
        dx = pos_ref[2 * j + 1] - my_col * N
        reach = (dy > -N) & (dx > -N) & (dy < N) & (dx < N)

        @pl.when(reach)
        def _():
            near_ref[2 * found] = dy
            near_ref[2 * found + 1] = dx

        return found + reach.astype(jnp.int32)

    lax.fori_loop(jnp.maximum(band - 1, 0) * 64, (band + 1) * 64, note, 0)


def deposit(sums, row, col, dr, dc, lane, halves):
    a, b = (pltpu.roll(z, dc, 1) for z in halves)
    hold = lane < dc
    zero = jnp.zeros_like(a)
    wide = jnp.concatenate(
        [jnp.where(hold, zero, a), jnp.where(hold, a, b), jnp.where(hold, b, zero)],
        axis=1,
    )
    tall = jnp.concatenate([wide, jnp.zeros((8, 3 * H), jnp.float32)], axis=0)
    tall = pltpu.roll(tall, dr, 0)
    spot = (pl.ds(pl.multiple_of(row, 8), STRIP + 8), pl.ds(col, 3 * H))
    sums[spot] = sums[spot] + tall


SMEM = pl.BlockSpec(memory_space=pltpu.SMEM)
VMEM = pl.BlockSpec(memory_space=pltpu.VMEM)
ANY = pl.BlockSpec(memory_space=pltpu.HBM)


def run_patterns(first, pos, place, ext, probe, gathered, high, low, sel):
    f32, bf16 = jnp.float32, jnp.bfloat16
    return pl.pallas_call(
        functools.partial(pattern_kernel, first),
        out_shape=(
            jax.ShapeDtypeStruct((2, 2 * N, 2 * N), f32),
            jax.ShapeDtypeStruct((3, 2, N, H), f32),
            jax.ShapeDtypeStruct((2 * NEAR,), jnp.int32),
        ),
        in_specs=[SMEM, SMEM, VMEM, VMEM, ANY, VMEM, VMEM, VMEM],
        out_specs=(VMEM, VMEM, SMEM),
        scratch_shapes=[
            pltpu.VMEM((N, N), bf16),
            pltpu.VMEM((N, N), f32),
            pltpu.VMEM((2, N, N), f32),
            pltpu.VMEM((2, N, N), f32),
            pltpu.VMEM((2, N, N), bf16),
            pltpu.VMEM((2, N, N), bf16),
            pltpu.VMEM((N, N), f32),
            pltpu.VMEM((N, N), f32),
            pltpu.SemaphoreType.DMA,
        ],
        compiler_params=pltpu.CompilerParams(vmem_limit_bytes=40 * 2**20),
        name="patterns",
    )(pos, place, ext, probe, gathered, high, low, sel)


MESH = pl.DeviceIdType.MESH


def whereabouts():
    row, col = lax.axis_index("row"), lax.axis_index("col")
    z, y = row // 2, (row % 2) * 2 + (col // 2) % 2
    x, core = col // 4, col % 2

    def device(z, y, x, core):
        return (z * 2 + y // 2, x * 4 + (y % 2) * 2 + core)

    return row, col, z, y, x, core, device


def greet(peers):
    barrier = pltpu.get_barrier_semaphore()
    for peer in peers:
        pl.semaphore_signal(barrier, inc=1, device_id=peer, device_id_type=MESH)
    pl.semaphore_wait(barrier, len(peers))


class Copies:
    def __init__(self, send_sem, recv_sem):
        self.send_sem, self.recv_sem, self.made = send_sem, recv_sem, []

    def make(self, src, dst, peer, k=None):
        if k is None:
            k = len(self.made)
            self.made.append(None)
        copy = pltpu.make_async_remote_copy(
            src_ref=src,
            dst_ref=dst,
            send_sem=self.send_sem.at[k],
            recv_sem=self.recv_sem.at[k],
            device_id=peer,
            device_id_type=MESH,
        )
        self.made[k] = copy
        return copy, k

    def send(self, src, dst, peer):
        copy, _ = self.make(src, dst, peer)
        copy.start()
        return copy


def around(row, col):
    left, right = lax.rem(col + 15, 16), lax.rem(col + 1, 16)
    up, down = lax.rem(row + 7, 8), lax.rem(row + 1, 8)
    return left, right, up, down


TOP, END = slice(0, N), slice(N, 2 * N)


class Halo:
    def __init__(self, copies, tile, ext, row, col, core):
        left, right, up, down = around(row, col)
        self.core = core
        self.below, _ = copies.make(tile, ext.at[:, END, TOP], (up, col))
        self.right, _ = copies.make(tile, ext.at[:, TOP, END], (row, left))
        corner = ext.at[:, END, END]
        self.diag, k = copies.make(tile, corner, (up, left))
        self.onward, _ = copies.make(ext.at[:, END, TOP], corner, (row, left), k)

    def start_sides(self):
        self.right.start()

        @pl.when(self.core == 0)
        def _():
            self.diag.start()

    def finish(self):
        self.below.wait_recv()

        @pl.when(self.core == 1)
        def _():
            self.onward.start()

        self.below.wait_send()
        self.right.wait()
        self.onward.wait()


def start_kernel(obj_ref, amps_ref, ext_ref, all_ref, send_sem, recv_sem, own_sem):
    row, col, z, y, x, core, device = whereabouts()
    left, right, up, down = around(row, col)
    twin = device(z, y, x, 1 - core)
    beside = device(z, y + 1 - 2 * (y % 2), x, core)
    ahead, behind = device(z, y, (x + 1) % 4, core), device(z, y, (x + 3) % 4, core)
    greet(
        [
            twin,
            beside,
            ahead,
            behind,
            (row, left),
            (row, right),
            (up, col),
            (down, col),
            (up, left),
            (down, right),
        ]
    )
    copies = Copies(send_sem, recv_sem)

    def block(x, ylo, first=0, count=4):
        c = (x % 4) * 4 + ylo * 2 + core
        return all_ref.at[pl.ds(c * 4 + first, count)]

    ylo = y % 2
    mine, other = block(x, ylo), block(x, 1 - ylo)
    to_beside = copies.send(amps_ref, mine, beside)
    to_ahead = copies.send(amps_ref, mine, ahead)
    to_behind = copies.send(amps_ref, mine, behind)
    halo = Halo(copies, obj_ref, ext_ref, row, col, core)
    halo.below.start()
    halo.start_sides()
    own = [
        pltpu.make_async_copy(amps_ref, mine, own_sem.at[0]),
        pltpu.make_async_copy(obj_ref, ext_ref.at[:, TOP, TOP], own_sem.at[1]),
    ]
    for copy in own:
        copy.start()
    rest = [copies.send(amps_ref, mine, twin)]
    to_beside.wait_recv()
    ahead_2 = copies.send(other, other, ahead)
    behind_2 = copies.send(other, other, behind)
    rest.append(copies.send(other, other, twin))
    far = []
    for low, high, side in ((to_ahead, to_behind, ylo), (ahead_2, behind_2, 1 - ylo)):
        low.wait_recv()
        part = block(x + 3, side, 0, 2)
        far.append((copies.send(part, part, ahead), block(x + 2, side, 0, 2)))
        whole = block(x + 3, side)
        rest.append(copies.send(whole, whole, twin))
        high.wait_recv()
        part = block(x + 1, side, 2, 2)
        far.append((copies.send(part, part, behind), block(x + 2, side, 2, 2)))
        whole = block(x + 1, side)
        rest.append(copies.send(whole, whole, twin))
    for copy, part in far:
        copy.wait_recv()
        rest.append(copies.send(part, part, twin))
    for copy in own:
        copy.wait()
    for copy in (to_beside, to_ahead, to_behind, ahead_2, behind_2):
        copy.wait_send()
    for copy, _ in far:
        copy.wait_send()
    for copy in rest:
        copy.wait()
    halo.finish()


def run_start(obj, amplitudes):
    count = 3 + 3 + 1 + 3 + 8 + 4
    return pl.pallas_call(
        start_kernel,
        out_shape=(
            jax.ShapeDtypeStruct((2, 2 * N, 2 * N), jnp.float32),
            jax.ShapeDtypeStruct((64, N, N), jnp.bfloat16),
        ),
        in_specs=[VMEM, ANY],
        out_specs=(VMEM, ANY),
        scratch_shapes=[
            pltpu.SemaphoreType.DMA((count,)),
            pltpu.SemaphoreType.DMA((count,)),
            pltpu.SemaphoreType.DMA((2,)),
        ],
        compiler_params=pltpu.CompilerParams(
            collective_id=1, has_side_effects=True, vmem_limit_bytes=16 * 2**20
        ),
        name="start",
    )(obj, amplitudes)


def exchange_kernel(
    last,
    sums_ref,
    near_ref,
    ext_ref,
    part_ref,
    old_ref,
    tile_ref,
    out_ref,
    from_left,
    from_above,
    corner,
    low,
    pair,
    half,
    from_x,
    quarter,
    from_z,
    small,
    from_y,
    weights,
    power_high,
    power_low,
    send_sem,
    recv_sem,
):
    row, col, z, y, x, core, device = whereabouts()
    left, right, up, down = around(row, col)
    twin = device(z, y, x, 1 - core)
    on_x = [device(z, y, (x + d) % 4, core) for d in (1, 2, 3)]
    on_y = [device(z, (y + d) % 4, x, core) for d in (1, 2, 3)]
    on_z = [device((z + d) % 4, y, x, core) for d in (1, 2, 3)]
    greet(
        [
            (row, left),
            (row, right),
            (up, col),
            (down, col),
            (up, left),
            (down, right),
            twin,
            *on_x,
            *on_y,
            *on_z,
        ]
    )
    copies = Copies(send_sem, recv_sem)

    def finish(group):
        for copy in group:
            copy.wait()

    def add_weights(start, stop):
        gap = lax.broadcasted_iota(jnp.int32, (N, N), 0) - lax.broadcasted_iota(
            jnp.int32, (N, N), 1
        )

        def add(i, _):
            dy, dx = near_ref[2 * i], near_ref[2 * i + 1]
            to_row = jnp.where(gap == dy, 1.0, 0.0).astype(jnp.bfloat16)
            to_col = jnp.where(gap == -dx, 1.0, 0.0).astype(jnp.bfloat16)
            a = mm(power_high[...], to_col).astype(jnp.bfloat16)
            b = mm(power_low[...], to_col).astype(jnp.bfloat16)
            weights[...] += mm(to_row, a) + mm(to_row, b)
            return 0

        lax.fori_loop(start, stop, add, 0)

    on_pair = copies.send(part_ref.at[:, 1 - core], pair, twin)
    edge = sums_ref.at[:, END, END]
    inside, k = copies.make(edge, corner, twin)
    outside, _ = copies.make(edge, corner, (down, right), k)
    down_sums, k = copies.make(sums_ref.at[:, END, TOP], from_above, (down, col))
    down_joint, _ = copies.make(low, from_above, (down, col), k)
    to_right, _ = copies.make(sums_ref.at[:, TOP, END], from_left, (row, right))

    @pl.when(core == 0)
    def _():
        inside.start()
        down_sums.start()

    weights[...] = jnp.zeros((N, N), jnp.float32)
    for k in range(2):
        cols = pl.ds(k * H, H)
        power = old_ref[0, k] * old_ref[0, k] + old_ref[1, k] * old_ref[1, k]
        power_high[:, cols], power_low[:, cols] = split(power)
    on_pair.wait()
    for q in range(3):
        half[q] = part_ref[q, core] + pair[q]
    group = [
        copies.send(
            half.at[:, pl.ds(pl.multiple_of((x + d) % 4 * 64, 64), 64), :],
            from_x.at[d - 1],
            on_x[d - 1],
        )
        for d in (1, 2, 3)
    ]

    @pl.when(core == 1)
    def _():
        inside.wait_recv()
        low[...] = sums_ref[:, END, TOP] + corner[...]
        down_joint.start()

    add_weights(0, 16)
    finish(group)
    mine = pl.ds(pl.multiple_of(x * 64, 64), 64)
    quarter[...] = (half[:, mine, :] + from_x[0]) + (from_x[1] + from_x[2])
    group = [
        copies.send(
            quarter.at[:, pl.ds(pl.multiple_of((z + d) % 4 * 16, 16), 16), :],
            from_z.at[d - 1],
            on_z[d - 1],
        )
        for d in (1, 2, 3)
    ]

    @pl.when(core == 1)
    def _():
        outside.start()

    to_right.start()
    add_weights(16, 24)
    finish(group)
    mine = pl.ds(pl.multiple_of(z * 16, 16), 16)
    small[...] = (quarter[:, mine, :] + from_z[0]) + (from_z[1] + from_z[2])
    group = [copies.send(small, from_y.at[y], peer) for peer in on_y]
    from_y[y] = small[...]
    add_weights(24, 32)

    def object_update():
        to_right.wait()
        down_sums.wait()

        @pl.when(core == 0)
        def _():
            outside.wait_recv()

        outside.wait_send()
        for r in range(0, N, STRIP):
            rows = pl.ds(r, STRIP)
            scale = 1.0 / (weights[rows, :] + object_regular)
            for q in range(2):
                total = sums_ref[q, rows, TOP] + from_left[q, rows, :]
                total = total + from_above[q, rows, :]
                total = total + jnp.where(core == 0, corner[q, rows, :], 0.0)
                tile_ref[q, rows, TOP] = ext_ref[q, rows, TOP] + total * scale

    if not last:
        object_update()
        halo = Halo(copies, tile_ref.at[:, TOP, TOP], tile_ref, row, col, core)
        halo.below.start()
    finish(group)
    total = (from_y[0] + from_y[1]) + (from_y[2] + from_y[3])
    rows = pl.ds(pl.multiple_of(x * 64 + z * 16, 16), 16)
    for q in range(2):
        out_ref[q, core, rows, :] = old_ref[q, core, rows, :] + total[q] / (
            total[2] + probe_regular
        )
    piece = out_ref.at[:, core, rows, :]
    finish([copies.send(piece, piece, peer) for peer in on_z])
    piece = out_ref.at[:, core, pl.ds(pl.multiple_of(x * 64, 64), 64), :]
    group = [copies.send(piece, piece, peer) for peer in on_x]
    if last:
        object_update()
    else:
        halo.start_sides()
    finish(group)
    piece = out_ref.at[:, core]
    to_twin = copies.send(piece, piece, twin)
    if not last:
        halo.finish()
    to_twin.wait()


def run_exchange(last, sums, near, ext, partials, probe):
    f32 = jnp.float32
    count = 4 + 9 + (0 if last else 3) + 7
    tile = (2, N, N) if last else (2, 2 * N, 2 * N)
    return pl.pallas_call(
        functools.partial(exchange_kernel, last),
        out_shape=(
            jax.ShapeDtypeStruct(tile, f32),
            jax.ShapeDtypeStruct((2, 2, N, H), f32),
        ),
        in_specs=[VMEM, SMEM, VMEM, VMEM, VMEM],
        out_specs=(VMEM, VMEM),
        scratch_shapes=[
            pltpu.VMEM((2, N, N), f32),
            pltpu.VMEM((2, N, N), f32),
            pltpu.VMEM((2, N, N), f32),
            pltpu.VMEM((2, N, N), f32),
            pltpu.VMEM((3, N, H), f32),
            pltpu.VMEM((3, N, H), f32),
            pltpu.VMEM((3, 3, 64, H), f32),
            pltpu.VMEM((3, 64, H), f32),
            pltpu.VMEM((3, 3, 16, H), f32),
            pltpu.VMEM((3, 16, H), f32),
            pltpu.VMEM((4, 3, 16, H), f32),
            pltpu.VMEM((N, N), f32),
            pltpu.VMEM((N, N), jnp.bfloat16),
            pltpu.VMEM((N, N), jnp.bfloat16),
            pltpu.SemaphoreType.DMA((count,)),
            pltpu.SemaphoreType.DMA((count,)),
        ],
        compiler_params=pltpu.CompilerParams(
            collective_id=3 if last else 2,
            has_side_effects=True,
            vmem_limit_bytes=32 * 2**20,
        ),
        name="finish" if last else "exchange",
    )(sums, near, ext, partials, probe)


def local(obj, probe, amplitudes, positions):
    place = jnp.stack([lax.axis_index("row"), lax.axis_index("col")]).astype(jnp.int32)
    pos = positions.reshape(-1)
    high, low = real_tables()
    sel = order_tables()
    illum = jnp.stack([probe[:, :, :H], probe[:, :, H:]], axis=1)
    ext, gathered = run_start(obj, amplitudes)
    near = None
    for sweep in range(ITERS):
        sums, partials, listed = run_patterns(
            sweep == 0, pos, place, ext, illum, gathered, high, low, sel
        )
        near = listed if sweep == 0 else near
        ext, illum = run_exchange(
            sweep == ITERS - 1, sums, near, ext, partials, illum
        )
    return ext, jnp.concatenate([illum[:, 0], illum[:, 1]], axis=2)


def solution(mesh):
    placed = (P(None, "row", "col"), P(), P(("row", "col"), None, None), P())
    return jax.shard_map(
        local,
        mesh=mesh,
        in_specs=placed,
        out_specs=(P(None, "row", "col"), P()),
        check_vma=False,
    )
```

```python
import functools

import jax
import jax.numpy as jnp
import numpy as np
from jax import lax
from jax.experimental import pallas as pl
from jax.experimental.pallas import tpu as pltpu
from jax.sharding import PartitionSpec as P

ITERS = 2
amplitude_floor = 0.1
object_regular = 0.5
probe_regular = 1.0

N = 256
NEAR = 32
FAR = 4096
H = 128
STRIP = 32


def real_tables():
    n = np.arange(H)
    out = []
    for odd in (0, 1):
        phase = (n[:, None] * (2 * n[None, :] + odd)) % N
        angle = phase * (2 * np.pi / N)
        re, im = np.cos(angle) / 16.0, -np.sin(angle) / 16.0
        full = np.block([[re, im], [-im, re]]).astype(np.float32)
        out += [full, full.T]
    full = jnp.asarray(np.stack(out))
    high = full.astype(jnp.bfloat16)
    low = (full - high.astype(jnp.float32)).astype(jnp.bfloat16)
    return high, low


def order_tables():
    order = np.concatenate([np.arange(0, N, 2), np.arange(1, N, 2)])
    sel = np.zeros((N, N), np.float32)
    sel[np.arange(N), order] = 1.0
    return jnp.asarray(np.stack([sel, sel.T])).astype(jnp.bfloat16)


def split(x):
    high = x.astype(jnp.bfloat16)
    low = (x - high.astype(jnp.float32)).astype(jnp.bfloat16)
    return high, low


def mm(a, b):
    return jnp.dot(a, b, preferred_element_type=jnp.float32)


def pattern_kernel(
    first,
    pos_ref,
    place_ref,
    ext,
    probe_ref,
    amps_ref,
    th_ref,
    tl_ref,
    sel_ref,
    sums_ref,
    part_ref,
    near_ref,
    todo,
    *work,
):
    band = place_ref[0]
    my_col = place_ref[1]
    for r in range(0, 2 * N, STRIP):
        for q in range(2):
            sums_ref[q, pl.ds(r, STRIP), :] = jnp.zeros((STRIP, 2 * N), jnp.float32)
    part_ref[...] = jnp.zeros_like(part_ref)

    lane = lax.broadcasted_iota(jnp.int32, (STRIP, H), 1)

    def process(spaces, j, top, left, valid):
        amp, win, psi, ah, al, ye, yo = spaces
        r8 = pl.multiple_of((top // 8) * 8, 8)
        dr = top - r8
        c128 = pl.multiple_of((left // H) * H, H)
        dc = left - c128

        def cut(s, _):
            r0 = s * STRIP
            w = []
            for q in range(2):
                block = ext[q, pl.ds(r8 + r0, STRIP + 8), pl.ds(c128, 3 * H)]
                block = pltpu.roll(block, lax.rem(STRIP + 8 - dr, STRIP + 8), 0)[:STRIP]
                turned = [
                    pltpu.roll(block[:, k * H : (k + 1) * H], lax.rem(H - dc, H), 1)
                    for k in range(3)
                ]
                keep = lane < H - dc
                w.append(
                    [
                        jnp.where(keep, turned[0], turned[1]),
                        jnp.where(keep, turned[1], turned[2]),
                    ]
                )
            rows = pl.ds(r0, STRIP)
            x = []
            for k in range(2):
                cols = pl.ds(k * H, H)
                wr, wi = w[0][k], w[1][k]
                win[0, rows, cols] = wr
                win[1, rows, cols] = wi
                pr, pi = probe_ref[0, k, rows, :], probe_ref[1, k, rows, :]
                er = pr * wr - pi * wi
                ei = pr * wi + pi * wr
                psi[0, rows, cols] = er
                psi[1, rows, cols] = ei
                x.append((er, ei))
            for k, z in enumerate(
                (
                    x[0][0] + x[1][0],
                    x[0][1] + x[1][1],
                    x[0][0] - x[1][0],
                    x[0][1] - x[1][1],
                )
            ):
                high, low = split(z)
                ah[k // 2, rows, pl.ds((k % 2) * H, H)] = high
                al[k // 2, rows, pl.ds((k % 2) * H, H)] = low
            return 0

        for s in range(N // STRIP):
            cut(s, 0)
        yield

        def right_apply(t):
            for k, out in ((0, ye), (1, yo)):
                th, tl = th_ref[2 * k + t], tl_ref[2 * k + t]
                out[...] = mm(ah[k], th) + mm(al[k], th) + mm(ah[k], tl)

        def left_apply(t):
            for k, out in ((0, ye), (1, yo)):
                th, tl = th_ref[2 * k + t], tl_ref[2 * k + t]
                out[...] = mm(th, ah[k]) + mm(th, al[k]) + mm(tl, ah[k])

        def put(k, rows, cols, z):
            high, low = split(z)
            ah[k, rows, cols] = high
            al[k, rows, cols] = low

        right_apply(0)
        yield

        def rows_forward(s, _):
            r0 = s * STRIP
            up, down = pl.ds(r0, STRIP), pl.ds(r0 + H, STRIP)
            for k, src in ((0, ye), (1, yo)):
                cols = pl.ds(k * H, H)
                for q in range(2):
                    part = pl.ds(q * H, H)
                    a, b = src[up, part], src[down, part]
                    dest = up if q == 0 else down
                    put(0, dest, cols, a + b)
                    put(1, dest, cols, a - b)
            return 0

        for s in range(H // STRIP):
            rows_forward(s, 0)
        yield
        left_apply(1)
        amp[...] = mm(mm(sel_ref[0], amps_ref[j]).astype(jnp.bfloat16), sel_ref[1])
        yield

        def modulus(s, _):
            r0 = s * STRIP
            up, down = pl.ds(r0, STRIP), pl.ds(r0 + H, STRIP)
            for k, src in ((0, ye), (1, yo)):
                re, im = src[up, :], src[down, :]
                m = amp[pl.ds(r0 + k * H, STRIP), :]
                f = m * lax.rsqrt(re * re + im * im + amplitude_floor)
                put(k, up, slice(None), re * f)
                put(k, down, slice(None), im * f)
            return 0

        for s in range(H // STRIP):
            modulus(s, 0)
        yield
        left_apply(0)
        yield

        def rows_back(s, _):
            r0 = s * STRIP
            up, down = pl.ds(r0, STRIP), pl.ds(r0 + H, STRIP)
            for q, src_rows in ((0, up), (1, down)):
                part = pl.ds(q * H, H)
                e, o = ye[src_rows, :], yo[src_rows, :]
                for dest, z in ((up, e + o), (down, e - o)):
                    put(0, dest, part, z[:, :H])
                    put(1, dest, part, z[:, H:])
            return 0

        for s in range(H // STRIP):
            rows_back(s, 0)
        yield
        right_apply(1)
        yield

        def finish(s, _):
            r0 = s * STRIP
            rows = pl.ds(r0, STRIP)
            e_re, e_im = ye[rows, :H], ye[rows, H:]
            o_re, o_im = yo[rows, :H], yo[rows, H:]
            term = [[], []]
            for k in range(2):
                cols = pl.ds(k * H, H)
                br = e_re + o_re if k == 0 else e_re - o_re
                bi = e_im + o_im if k == 0 else e_im - o_im
                cr = (br - psi[0, rows, cols]) * valid
                ci = (bi - psi[1, rows, cols]) * valid
                pr, pi = probe_ref[0, k, rows, :], probe_ref[1, k, rows, :]
                wr, wi = win[0, rows, cols], win[1, rows, cols]
                term[0].append(pr * cr + pi * ci)
                term[1].append(pr * ci - pi * cr)
                part_ref[0, k, rows, :] += wr * cr + wi * ci
                part_ref[1, k, rows, :] += wr * ci - wi * cr
                part_ref[2, k, rows, :] += (wr * wr + wi * wi) * valid
            for q in range(2):
                deposit(sums_ref.at[q], r8 + r0, c128, dr, dc, lane, term[q])
            return 0

        for s in range(N // STRIP):
            finish(s, 0)
        yield

    def visit(i, found):
        j = band * 64 + i
        mine = pos_ref[2 * j + 1] // N == my_col

        @pl.when(mine)
        def _():
            todo[found] = i

        return found + mine.astype(jnp.int32)

    count = lax.fori_loop(0, 64, visit, 0)

    def pair(k, _):
        lanes = []
        for half in range(2):
            at = 2 * k + half
            i = todo[jnp.minimum(at, count - 1)]
            j = band * 64 + i
            valid = (at < count).astype(jnp.float32)
            lanes.append(
                process(
                    work[7 * half : 7 * half + 7],
                    i,
                    pos_ref[2 * j] - band * N,
                    pos_ref[2 * j + 1] - my_col * N,
                    valid,
                )
            )
        next(lanes[0])
        alive = [True, True]
        while any(alive):
            for half in (1, 0):
                if alive[half]:
                    alive[half] = next(lanes[half], 0) is None
        return 0

    lax.fori_loop(0, (count + 1) // 2, pair, 0)
    if not first:
        return

    for k in range(2 * NEAR):
        near_ref[k] = FAR

    def note(j, found):
        dy = pos_ref[2 * j] - band * N
        dx = pos_ref[2 * j + 1] - my_col * N
        reach = (dy > -N) & (dx > -N) & (dy < N) & (dx < N)

        @pl.when(reach)
        def _():
            near_ref[2 * found] = dy
            near_ref[2 * found + 1] = dx

        return found + reach.astype(jnp.int32)

    lax.fori_loop(jnp.maximum(band - 1, 0) * 64, (band + 1) * 64, note, 0)


def deposit(sums, row, col, dr, dc, lane, halves):
    a, b = (pltpu.roll(z, dc, 1) for z in halves)
    hold = lane < dc
    zero = jnp.zeros_like(a)
    wide = jnp.concatenate(
        [jnp.where(hold, zero, a), jnp.where(hold, a, b), jnp.where(hold, b, zero)],
        axis=1,
    )
    tall = jnp.concatenate([wide, jnp.zeros((8, 3 * H), jnp.float32)], axis=0)
    tall = pltpu.roll(tall, dr, 0)
    spot = (pl.ds(pl.multiple_of(row, 8), STRIP + 8), pl.ds(col, 3 * H))
    sums[spot] = sums[spot] + tall


SMEM = pl.BlockSpec(memory_space=pltpu.SMEM)
VMEM = pl.BlockSpec(memory_space=pltpu.VMEM)
ANY = pl.BlockSpec(memory_space=pltpu.HBM)


def run_patterns(first, pos, place, ext, probe, gathered, high, low, sel):
    f32, bf16 = jnp.float32, jnp.bfloat16
    return pl.pallas_call(
        functools.partial(pattern_kernel, first),
        out_shape=(
            jax.ShapeDtypeStruct((2, 2 * N, 2 * N), f32),
            jax.ShapeDtypeStruct((3, 2, N, H), f32),
            jax.ShapeDtypeStruct((2 * NEAR,), jnp.int32),
        ),
        in_specs=[SMEM, SMEM, VMEM, VMEM, VMEM, VMEM, VMEM, VMEM],
        out_specs=(VMEM, VMEM, SMEM),
        scratch_shapes=[
            pltpu.SMEM((64,), jnp.int32),
            *2
            * (
                pltpu.VMEM((N, N), f32),
                pltpu.VMEM((2, N, N), f32),
                pltpu.VMEM((2, N, N), f32),
                pltpu.VMEM((2, N, N), bf16),
                pltpu.VMEM((2, N, N), bf16),
                pltpu.VMEM((N, N), f32),
                pltpu.VMEM((N, N), f32),
            ),
        ],
        compiler_params=pltpu.CompilerParams(vmem_limit_bytes=24 * 2**20),
        name="patterns",
    )(pos, place, ext, probe, gathered, high, low, sel)


MESH = pl.DeviceIdType.MESH


def whereabouts():
    row, col = lax.axis_index("row"), lax.axis_index("col")
    z, y = row // 2, (row % 2) * 2 + (col // 2) % 2
    x, core = col // 4, col % 2

    def device(z, y, x, core):
        return (z * 2 + y // 2, x * 4 + (y % 2) * 2 + core)

    return row, col, z, y, x, core, device


def greet(peers):
    barrier = pltpu.get_barrier_semaphore()
    for peer in peers:
        pl.semaphore_signal(barrier, inc=1, device_id=peer, device_id_type=MESH)
    pl.semaphore_wait(barrier, len(peers))


class Copies:
    def __init__(self, send_sem, recv_sem):
        self.send_sem, self.recv_sem, self.made = send_sem, recv_sem, []

    def make(self, src, dst, peer, k=None):
        if k is None:
            k = len(self.made)
            self.made.append(None)
        copy = pltpu.make_async_remote_copy(
            src_ref=src,
            dst_ref=dst,
            send_sem=self.send_sem.at[k],
            recv_sem=self.recv_sem.at[k],
            device_id=peer,
            device_id_type=MESH,
        )
        self.made[k] = copy
        return copy, k

    def send(self, src, dst, peer):
        copy, _ = self.make(src, dst, peer)
        copy.start()
        return copy


def around(row, col):
    left, right = lax.rem(col + 15, 16), lax.rem(col + 1, 16)
    up, down = lax.rem(row + 7, 8), lax.rem(row + 1, 8)
    return left, right, up, down


TOP, END = slice(0, N), slice(N, 2 * N)


class Bulk:
    def __init__(self, copies, src, dst, peer, k=None):
        self.whole, self.k = copies.make(src, dst, peer, k)
        self.copies, self.src, self.dst, self.peer = copies, src, dst, peer

    def start(self, first=0, stop=4):
        for part in range(first, stop):
            rows = pl.ds(part * 64, 64)
            self.copies.make(
                self.src.at[:, rows], self.dst.at[:, rows], self.peer, self.k
            )[0].start()


class Halo:
    def __init__(self, copies, tile, ext, row, col, core):
        left, right, up, down = around(row, col)
        self.core = core
        self.below = Bulk(copies, tile, ext.at[:, END, TOP], (up, col))
        self.right = Bulk(copies, tile, ext.at[:, TOP, END], (row, left))
        corner = ext.at[:, END, END]
        self.diag = Bulk(copies, tile, corner, (up, left))
        self.onward, _ = copies.make(
            ext.at[:, END, TOP], corner, (row, left), self.diag.k
        )

    def start_sides(self, first=0, stop=4):
        self.right.start(first, stop)

        @pl.when(self.core == 0)
        def _():
            self.diag.start(first, stop)

    def finish(self):
        self.below.whole.wait_recv()

        @pl.when(self.core == 1)
        def _():
            self.onward.start()

        self.below.whole.wait_send()
        self.right.whole.wait()
        self.onward.wait()


def start_kernel(obj_ref, amps_ref, ext_ref, all_ref, send_sem, recv_sem, own_sem):
    row, col, z, y, x, core, device = whereabouts()
    left, right, up, down = around(row, col)
    twin = device(z, y, x, 1 - core)
    beside = device(z, y + 1 - 2 * (y % 2), x, core)
    ahead, behind = device(z, y, (x + 1) % 4, core), device(z, y, (x + 3) % 4, core)
    greet(
        [
            twin,
            beside,
            ahead,
            behind,
            (row, left),
            (row, right),
            (up, col),
            (down, col),
            (up, left),
            (down, right),
        ]
    )
    copies = Copies(send_sem, recv_sem)

    def block(x, ylo, first=0, count=4):
        c = (x % 4) * 4 + ylo * 2 + core
        return all_ref.at[pl.ds(c * 4 + first, count)]

    ylo = y % 2
    mine, other = block(x, ylo), block(x, 1 - ylo)
    to_beside = copies.send(amps_ref, mine, beside)
    to_ahead = copies.send(amps_ref, mine, ahead)
    to_behind = copies.send(amps_ref, mine, behind)
    halo = Halo(copies, obj_ref, ext_ref, row, col, core)
    own = [
        pltpu.make_async_copy(amps_ref, mine, own_sem.at[0]),
        pltpu.make_async_copy(obj_ref, ext_ref.at[:, TOP, TOP], own_sem.at[1]),
    ]
    for copy in own:
        copy.start()
    rest = [copies.send(amps_ref, mine, twin)]
    to_beside.wait_recv()
    ahead_2 = copies.send(other, other, ahead)
    behind_2 = copies.send(other, other, behind)
    halo.below.start()
    halo.start_sides()
    rest.append(copies.send(other, other, twin))
    far = []
    for low, high, side in ((to_ahead, to_behind, ylo), (ahead_2, behind_2, 1 - ylo)):
        low.wait_recv()
        part = block(x + 3, side, 0, 2)
        far.append((copies.send(part, part, ahead), block(x + 2, side, 0, 2)))
        whole = block(x + 3, side)
        rest.append(copies.send(whole, whole, twin))
        high.wait_recv()
        part = block(x + 1, side, 2, 2)
        far.append((copies.send(part, part, behind), block(x + 2, side, 2, 2)))
        whole = block(x + 1, side)
        rest.append(copies.send(whole, whole, twin))
    for copy, part in far:
        copy.wait_recv()
        rest.append(copies.send(part, part, twin))
    for copy in own:
        copy.wait()
    for copy in (to_beside, to_ahead, to_behind, ahead_2, behind_2):
        copy.wait_send()
    for copy, _ in far:
        copy.wait_send()
    for copy in rest:
        copy.wait()
    halo.finish()


def run_start(obj, amplitudes):
    count = 3 + 3 + 1 + 3 + 8 + 4
    return pl.pallas_call(
        start_kernel,
        out_shape=(
            jax.ShapeDtypeStruct((2, 2 * N, 2 * N), jnp.float32),
            jax.ShapeDtypeStruct((64, N, N), jnp.bfloat16),
        ),
        in_specs=[VMEM, ANY],
        out_specs=(VMEM, ANY),
        scratch_shapes=[
            pltpu.SemaphoreType.DMA((count,)),
            pltpu.SemaphoreType.DMA((count,)),
            pltpu.SemaphoreType.DMA((2,)),
        ],
        compiler_params=pltpu.CompilerParams(
            collective_id=1, has_side_effects=True, vmem_limit_bytes=16 * 2**20
        ),
        name="start",
    )(obj, amplitudes)


def exchange_kernel(
    last,
    sums_ref,
    near_ref,
    ext_ref,
    part_ref,
    old_ref,
    tile_ref,
    out_ref,
    from_left,
    from_above,
    corner,
    low,
    pair,
    half,
    from_x,
    quarter,
    from_z,
    small,
    from_y,
    weights,
    power_high,
    power_low,
    send_sem,
    recv_sem,
):
    row, col, z, y, x, core, device = whereabouts()
    left, right, up, down = around(row, col)
    twin = device(z, y, x, 1 - core)
    on_x = [device(z, y, (x + d) % 4, core) for d in (1, 2, 3)]
    on_y = [device(z, (y + d) % 4, x, core) for d in (1, 2, 3)]
    on_z = [device((z + d) % 4, y, x, core) for d in (1, 2, 3)]
    greet(
        [
            (row, left),
            (row, right),
            (up, col),
            (down, col),
            (up, left),
            (down, right),
            twin,
            *on_x,
            *on_y,
            *on_z,
        ]
    )
    copies = Copies(send_sem, recv_sem)

    def finish(group):
        for copy in group:
            copy.wait()

    def add_weights(start, stop):
        gap = lax.broadcasted_iota(jnp.int32, (N, N), 0) - lax.broadcasted_iota(
            jnp.int32, (N, N), 1
        )

        def add(i, _):
            dy, dx = near_ref[2 * i], near_ref[2 * i + 1]
            to_row = jnp.where(gap == dy, 1.0, 0.0).astype(jnp.bfloat16)
            to_col = jnp.where(gap == -dx, 1.0, 0.0).astype(jnp.bfloat16)
            a = mm(power_high[...], to_col).astype(jnp.bfloat16)
            b = mm(power_low[...], to_col).astype(jnp.bfloat16)
            weights[...] += mm(to_row, a) + mm(to_row, b)
            return 0

        lax.fori_loop(start, stop, add, 0, unroll=4)

    on_pair = copies.send(part_ref.at[:, 1 - core], pair, twin)
    edge = sums_ref.at[:, END, END]
    inside, k = copies.make(edge, corner, twin)
    outside = Bulk(copies, edge, corner, (down, right), k)
    down_sums = Bulk(copies, sums_ref.at[:, END, TOP], from_above, (down, col))
    down_joint = Bulk(copies, low, from_above, (down, col), down_sums.k)
    to_right = Bulk(copies, sums_ref.at[:, TOP, END], from_left, (row, right))

    def send_down(first, stop):
        @pl.when(core == 0)
        def _():
            down_sums.start(first, stop)

        @pl.when(core == 1)
        def _():
            down_joint.start(first, stop)

    def send_right(first, stop):
        @pl.when(core == 1)
        def _():
            outside.start(first, stop)

        to_right.start(first, stop)

    @pl.when(core == 0)
    def _():
        inside.start()

    weights[...] = jnp.zeros((N, N), jnp.float32)
    for k in range(2):
        cols = pl.ds(k * H, H)
        power = old_ref[0, k] * old_ref[0, k] + old_ref[1, k] * old_ref[1, k]
        power_high[:, cols], power_low[:, cols] = split(power)
    on_pair.wait()
    for q in range(3):
        half[q] = part_ref[q, core] + pair[q]
    group = [
        copies.send(
            half.at[:, pl.ds(pl.multiple_of((x + d) % 4 * 64, 64), 64), :],
            from_x.at[d - 1],
            on_x[d - 1],
        )
        for d in (1, 2, 3)
    ]

    @pl.when(core == 1)
    def _():
        inside.wait_recv()
        low[...] = sums_ref[:, END, TOP] + corner[...]

    send_down(0, 2)
    add_weights(0, 16)
    finish(group)
    mine = pl.ds(pl.multiple_of(x * 64, 64), 64)
    quarter[...] = (half[:, mine, :] + from_x[0]) + (from_x[1] + from_x[2])
    group = [
        copies.send(
            quarter.at[:, pl.ds(pl.multiple_of((z + d) % 4 * 16, 16), 16), :],
            from_z.at[d - 1],
            on_z[d - 1],
        )
        for d in (1, 2, 3)
    ]

    send_right(0, 2)
    add_weights(16, 24)
    finish(group)
    mine = pl.ds(pl.multiple_of(z * 16, 16), 16)
    small[...] = (quarter[:, mine, :] + from_z[0]) + (from_z[1] + from_z[2])
    group = [copies.send(small, from_y.at[y], peer) for peer in on_y]
    from_y[y] = small[...]
    send_down(2, 3 if last else 4)
    send_right(2, 3 if last else 4)
    add_weights(24, 32)

    def object_update():
        to_right.whole.wait()
        down_sums.whole.wait()

        @pl.when(core == 0)
        def _():
            outside.whole.wait_recv()

        outside.whole.wait_send()
        for r in range(0, N, STRIP):
            rows = pl.ds(r, STRIP)
            scale = 1.0 / (weights[rows, :] + object_regular)
            for q in range(2):
                total = sums_ref[q, rows, TOP] + from_left[q, rows, :]
                total = total + from_above[q, rows, :]
                total = total + jnp.where(core == 0, corner[q, rows, :], 0.0)
                tile_ref[q, rows, TOP] = ext_ref[q, rows, TOP] + total * scale

    finish(group)
    total = (from_y[0] + from_y[1]) + (from_y[2] + from_y[3])
    rows = pl.ds(pl.multiple_of(x * 64 + z * 16, 16), 16)
    for q in range(2):
        out_ref[q, core, rows, :] = old_ref[q, core, rows, :] + total[q] / (
            total[2] + probe_regular
        )
    piece = out_ref.at[:, core, rows, :]
    group = [copies.send(piece, piece, peer) for peer in on_z]
    if last:
        send_down(3, 4)
        send_right(3, 4)
    else:
        object_update()
        halo = Halo(copies, tile_ref.at[:, TOP, TOP], tile_ref, row, col, core)
        halo.below.start()
    finish(group)
    piece = out_ref.at[:, core, pl.ds(pl.multiple_of(x * 64, 64), 64), :]
    group = [copies.send(piece, piece, peer) for peer in on_x]
    if not last:
        halo.start_sides()
    finish(group)
    piece = out_ref.at[:, core]
    to_twin = copies.send(piece, piece, twin)
    if last:
        object_update()
    else:
        halo.finish()
    to_twin.wait()


def run_exchange(last, sums, near, ext, partials, probe):
    f32 = jnp.float32
    count = 4 + 9 + (0 if last else 3) + 7
    tile = (2, N, N) if last else (2, 2 * N, 2 * N)
    return pl.pallas_call(
        functools.partial(exchange_kernel, last),
        out_shape=(
            jax.ShapeDtypeStruct(tile, f32),
            jax.ShapeDtypeStruct((2, 2, N, H), f32),
        ),
        in_specs=[VMEM, SMEM, VMEM, VMEM, VMEM],
        out_specs=(VMEM, VMEM),
        scratch_shapes=[
            pltpu.VMEM((2, N, N), f32),
            pltpu.VMEM((2, N, N), f32),
            pltpu.VMEM((2, N, N), f32),
            pltpu.VMEM((2, N, N), f32),
            pltpu.VMEM((3, N, H), f32),
            pltpu.VMEM((3, N, H), f32),
            pltpu.VMEM((3, 3, 64, H), f32),
            pltpu.VMEM((3, 64, H), f32),
            pltpu.VMEM((3, 3, 16, H), f32),
            pltpu.VMEM((3, 16, H), f32),
            pltpu.VMEM((4, 3, 16, H), f32),
            pltpu.VMEM((N, N), f32),
            pltpu.VMEM((N, N), jnp.bfloat16),
            pltpu.VMEM((N, N), jnp.bfloat16),
            pltpu.SemaphoreType.DMA((count,)),
            pltpu.SemaphoreType.DMA((count,)),
        ],
        compiler_params=pltpu.CompilerParams(
            collective_id=3 if last else 2,
            has_side_effects=True,
            vmem_limit_bytes=14 * 2**20,
        ),
        name="finish" if last else "exchange",
    )(sums, near, ext, partials, probe)


def local(obj, probe, amplitudes, positions):
    place = jnp.stack([lax.axis_index("row"), lax.axis_index("col")]).astype(jnp.int32)
    pos = positions.reshape(-1)
    high, low = real_tables()
    sel = order_tables()
    illum = jnp.stack([probe[:, :, :H], probe[:, :, H:]], axis=1)
    ext, gathered = run_start(obj, amplitudes)
    near = None
    for sweep in range(ITERS):
        sums, partials, listed = run_patterns(
            sweep == 0, pos, place, ext, illum, gathered, high, low, sel
        )
        near = listed if sweep == 0 else near
        ext, illum = run_exchange(
            sweep == ITERS - 1, sums, near, ext, partials, illum
        )
    return ext, jnp.concatenate([illum[:, 0], illum[:, 1]], axis=2)


def solution(mesh):
    placed = (P(None, "row", "col"), P(), P(("row", "col"), None, None), P())
    return jax.shard_map(
        local,
        mesh=mesh,
        in_specs=placed,
        out_specs=(P(None, "row", "col"), P()),
        check_vma=False,
    )
```

```python
import functools

import jax
import jax.numpy as jnp
import numpy as np
from jax import lax
from jax.experimental import pallas as pl
from jax.experimental.pallas import tpu as pltpu
from jax.sharding import PartitionSpec as P

ITERS = 2
amplitude_floor = 0.1
object_regular = 0.5
probe_regular = 1.0

N = 256
NEAR = 32
FAR = 4096
H = 128
STRIP = 32


def real_tables():
    n = np.arange(H)
    out = []
    for odd in (0, 1):
        phase = (n[:, None] * (2 * n[None, :] + odd)) % N
        angle = phase * (2 * np.pi / N)
        re, im = np.cos(angle) / 16.0, -np.sin(angle) / 16.0
        full = np.block([[re, im], [-im, re]]).astype(np.float32)
        out += [full, full.T]
    full = jnp.asarray(np.stack(out))
    high = full.astype(jnp.bfloat16)
    low = (full - high.astype(jnp.float32)).astype(jnp.bfloat16)
    return high, low


def order_tables():
    order = np.concatenate([np.arange(0, N, 2), np.arange(1, N, 2)])
    sel = np.zeros((N, N), np.float32)
    sel[np.arange(N), order] = 1.0
    return jnp.asarray(np.stack([sel, sel.T])).astype(jnp.bfloat16)


def split(x):
    high = x.astype(jnp.bfloat16)
    low = (x - high.astype(jnp.float32)).astype(jnp.bfloat16)
    return high, low


def mm(a, b):
    return jnp.dot(a, b, preferred_element_type=jnp.float32)


def pattern_kernel(
    first,
    pos_ref,
    place_ref,
    ext,
    probe_ref,
    amps_ref,
    th_ref,
    tl_ref,
    sel_ref,
    sums_ref,
    part_ref,
    near_ref,
    todo,
    *work,
):
    band = place_ref[0]
    my_col = place_ref[1]
    for r in range(0, 2 * N, STRIP):
        for q in range(2):
            sums_ref[q, pl.ds(r, STRIP), :] = jnp.zeros((STRIP, 2 * N), jnp.float32)
    part_ref[...] = jnp.zeros_like(part_ref)

    lane = lax.broadcasted_iota(jnp.int32, (STRIP, H), 1)

    def process(spaces, j, top, left, valid):
        amp, win, psi, ah, al, ye, yo = spaces
        r8 = pl.multiple_of((top // 8) * 8, 8)
        dr = top - r8
        c128 = pl.multiple_of((left // H) * H, H)
        dc = left - c128

        def cut(s, _):
            r0 = s * STRIP
            w = []
            for q in range(2):
                block = ext[q, pl.ds(r8 + r0, STRIP + 8), pl.ds(c128, 3 * H)]
                block = pltpu.roll(block, lax.rem(STRIP + 8 - dr, STRIP + 8), 0)[:STRIP]
                turned = [
                    pltpu.roll(block[:, k * H : (k + 1) * H], lax.rem(H - dc, H), 1)
                    for k in range(3)
                ]
                keep = lane < H - dc
                w.append(
                    [
                        jnp.where(keep, turned[0], turned[1]),
                        jnp.where(keep, turned[1], turned[2]),
                    ]
                )
            rows = pl.ds(r0, STRIP)
            x = []
            for k in range(2):
                cols = pl.ds(k * H, H)
                wr, wi = w[0][k], w[1][k]
                win[0, rows, cols] = wr
                win[1, rows, cols] = wi
                pr, pi = probe_ref[0, k, rows, :], probe_ref[1, k, rows, :]
                er = pr * wr - pi * wi
                ei = pr * wi + pi * wr
                psi[0, rows, cols] = er
                psi[1, rows, cols] = ei
                x.append((er, ei))
            for k, z in enumerate(
                (
                    x[0][0] + x[1][0],
                    x[0][1] + x[1][1],
                    x[0][0] - x[1][0],
                    x[0][1] - x[1][1],
                )
            ):
                high, low = split(z)
                ah[k // 2, rows, pl.ds((k % 2) * H, H)] = high
                al[k // 2, rows, pl.ds((k % 2) * H, H)] = low
            return 0

        for s in range(N // STRIP):
            cut(s, 0)
        yield

        def right_apply(t):
            for k, out in ((0, ye), (1, yo)):
                th, tl = th_ref[2 * k + t], tl_ref[2 * k + t]
                out[...] = mm(ah[k], th) + mm(al[k], th) + mm(ah[k], tl)

        def left_apply(t):
            for k, out in ((0, ye), (1, yo)):
                th, tl = th_ref[2 * k + t], tl_ref[2 * k + t]
                out[...] = mm(th, ah[k]) + mm(th, al[k]) + mm(tl, ah[k])

        def put(k, rows, cols, z):
            high, low = split(z)
            ah[k, rows, cols] = high
            al[k, rows, cols] = low

        right_apply(0)
        yield

        def rows_forward(s, _):
            r0 = s * STRIP
            up, down = pl.ds(r0, STRIP), pl.ds(r0 + H, STRIP)
            for k, src in ((0, ye), (1, yo)):
                cols = pl.ds(k * H, H)
                for q in range(2):
                    part = pl.ds(q * H, H)
                    a, b = src[up, part], src[down, part]
                    dest = up if q == 0 else down
                    put(0, dest, cols, a + b)
                    put(1, dest, cols, a - b)
            return 0

        for s in range(H // STRIP):
            rows_forward(s, 0)
        yield
        left_apply(1)
        amp[...] = mm(mm(sel_ref[0], amps_ref[j]).astype(jnp.bfloat16), sel_ref[1])
        yield

        def modulus(s, _):
            r0 = s * STRIP
            up, down = pl.ds(r0, STRIP), pl.ds(r0 + H, STRIP)
            for k, src in ((0, ye), (1, yo)):
                re, im = src[up, :], src[down, :]
                m = amp[pl.ds(r0 + k * H, STRIP), :]
                f = m * lax.rsqrt(re * re + im * im + amplitude_floor)
                put(k, up, slice(None), re * f)
                put(k, down, slice(None), im * f)
            return 0

        for s in range(H // STRIP):
            modulus(s, 0)
        yield
        left_apply(0)
        yield

        def rows_back(s, _):
            r0 = s * STRIP
            up, down = pl.ds(r0, STRIP), pl.ds(r0 + H, STRIP)
            for q, src_rows in ((0, up), (1, down)):
                part = pl.ds(q * H, H)
                e, o = ye[src_rows, :], yo[src_rows, :]
                for dest, z in ((up, e + o), (down, e - o)):
                    put(0, dest, part, z[:, :H])
                    put(1, dest, part, z[:, H:])
            return 0

        for s in range(H // STRIP):
            rows_back(s, 0)
        yield
        right_apply(1)
        yield

        def finish(s, _):
            r0 = s * STRIP
            rows = pl.ds(r0, STRIP)
            e_re, e_im = ye[rows, :H], ye[rows, H:]
            o_re, o_im = yo[rows, :H], yo[rows, H:]
            term = [[], []]
            for k in range(2):
                cols = pl.ds(k * H, H)
                br = e_re + o_re if k == 0 else e_re - o_re
                bi = e_im + o_im if k == 0 else e_im - o_im
                cr = (br - psi[0, rows, cols]) * valid
                ci = (bi - psi[1, rows, cols]) * valid
                pr, pi = probe_ref[0, k, rows, :], probe_ref[1, k, rows, :]
                wr, wi = win[0, rows, cols], win[1, rows, cols]
                term[0].append(pr * cr + pi * ci)
                term[1].append(pr * ci - pi * cr)
                part_ref[0, k, rows, :] += wr * cr + wi * ci
                part_ref[1, k, rows, :] += wr * ci - wi * cr
                part_ref[2, k, rows, :] += (wr * wr + wi * wi) * valid
            for q in range(2):
                deposit(sums_ref.at[q], r8 + r0, c128, dr, dc, lane, term[q])
            return 0

        for s in range(N // STRIP):
            finish(s, 0)
        yield

    def visit(i, found):
        j = band * 64 + i
        mine = pos_ref[2 * j + 1] // N == my_col

        @pl.when(mine)
        def _():
            todo[found] = i

        return found + mine.astype(jnp.int32)

    count = lax.fori_loop(0, 64, visit, 0)

    def pair(k, _):
        lanes = []
        for half in range(2):
            at = 2 * k + half
            i = todo[jnp.minimum(at, count - 1)]
            j = band * 64 + i
            valid = (at < count).astype(jnp.float32)
            lanes.append(
                process(
                    work[7 * half : 7 * half + 7],
                    i,
                    pos_ref[2 * j] - band * N,
                    pos_ref[2 * j + 1] - my_col * N,
                    valid,
                )
            )
        next(lanes[0])
        alive = [True, True]
        while any(alive):
            for half in (1, 0):
                if alive[half]:
                    alive[half] = next(lanes[half], 0) is None
        return 0

    lax.fori_loop(0, (count + 1) // 2, pair, 0)
    if not first:
        return

    for k in range(2 * NEAR):
        near_ref[k] = FAR

    def note(j, found):
        dy = pos_ref[2 * j] - band * N
        dx = pos_ref[2 * j + 1] - my_col * N
        reach = (dy > -N) & (dx > -N) & (dy < N) & (dx < N)

        @pl.when(reach)
        def _():
            near_ref[2 * found] = dy
            near_ref[2 * found + 1] = dx

        return found + reach.astype(jnp.int32)

    lax.fori_loop(jnp.maximum(band - 1, 0) * 64, (band + 1) * 64, note, 0)


def deposit(sums, row, col, dr, dc, lane, halves):
    a, b = (pltpu.roll(z, dc, 1) for z in halves)
    hold = lane < dc
    zero = jnp.zeros_like(a)
    wide = jnp.concatenate(
        [jnp.where(hold, zero, a), jnp.where(hold, a, b), jnp.where(hold, b, zero)],
        axis=1,
    )
    tall = jnp.concatenate([wide, jnp.zeros((8, 3 * H), jnp.float32)], axis=0)
    tall = pltpu.roll(tall, dr, 0)
    spot = (pl.ds(pl.multiple_of(row, 8), STRIP + 8), pl.ds(col, 3 * H))
    sums[spot] = sums[spot] + tall


SMEM = pl.BlockSpec(memory_space=pltpu.SMEM)
VMEM = pl.BlockSpec(memory_space=pltpu.VMEM)
ANY = pl.BlockSpec(memory_space=pltpu.HBM)


def run_patterns(first, pos, place, ext, probe, gathered, high, low, sel):
    f32, bf16 = jnp.float32, jnp.bfloat16
    return pl.pallas_call(
        functools.partial(pattern_kernel, first),
        out_shape=(
            jax.ShapeDtypeStruct((2, 2 * N, 2 * N), f32),
            jax.ShapeDtypeStruct((3, 2, N, H), f32),
            jax.ShapeDtypeStruct((2 * NEAR,), jnp.int32),
        ),
        in_specs=[SMEM, SMEM, VMEM, VMEM, VMEM, VMEM, VMEM, VMEM],
        out_specs=(VMEM, VMEM, SMEM),
        scratch_shapes=[
            pltpu.SMEM((64,), jnp.int32),
            *2
            * (
                pltpu.VMEM((N, N), f32),
                pltpu.VMEM((2, N, N), f32),
                pltpu.VMEM((2, N, N), f32),
                pltpu.VMEM((2, N, N), bf16),
                pltpu.VMEM((2, N, N), bf16),
                pltpu.VMEM((N, N), f32),
                pltpu.VMEM((N, N), f32),
            ),
        ],
        compiler_params=pltpu.CompilerParams(vmem_limit_bytes=24 * 2**20),
        name="patterns",
    )(pos, place, ext, probe, gathered, high, low, sel)


MESH = pl.DeviceIdType.MESH


def whereabouts():
    row, col = lax.axis_index("row"), lax.axis_index("col")
    z, y = row // 2, (row % 2) * 2 + (col // 2) % 2
    x, core = col // 4, col % 2

    def device(z, y, x, core):
        return (z * 2 + y // 2, x * 4 + (y % 2) * 2 + core)

    return row, col, z, y, x, core, device


def greet(peers):
    barrier = pltpu.get_barrier_semaphore()
    for peer in peers:
        pl.semaphore_signal(barrier, inc=1, device_id=peer, device_id_type=MESH)
    pl.semaphore_wait(barrier, len(peers))


class Copies:
    def __init__(self, send_sem, recv_sem):
        self.send_sem, self.recv_sem, self.made = send_sem, recv_sem, []

    def make(self, src, dst, peer, k=None):
        if k is None:
            k = len(self.made)
            self.made.append(None)
        copy = pltpu.make_async_remote_copy(
            src_ref=src,
            dst_ref=dst,
            send_sem=self.send_sem.at[k],
            recv_sem=self.recv_sem.at[k],
            device_id=peer,
            device_id_type=MESH,
        )
        self.made[k] = copy
        return copy, k

    def send(self, src, dst, peer):
        copy, _ = self.make(src, dst, peer)
        copy.start()
        return copy


def around(row, col):
    left, right = lax.rem(col + 15, 16), lax.rem(col + 1, 16)
    up, down = lax.rem(row + 7, 8), lax.rem(row + 1, 8)
    return left, right, up, down


TOP, END = slice(0, N), slice(N, 2 * N)


class Bulk:
    def __init__(self, copies, src, dst, peer, k=None):
        self.whole, self.k = copies.make(src, dst, peer, k)
        self.copies, self.src, self.dst, self.peer = copies, src, dst, peer

    def start(self, first=0, stop=4):
        for part in range(first, stop):
            rows = pl.ds(part * 64, 64)
            self.copies.make(
                self.src.at[:, rows], self.dst.at[:, rows], self.peer, self.k
            )[0].start()


class Halo:
    def __init__(self, copies, tile, ext, row, col, core):
        left, right, up, down = around(row, col)
        self.core = core
        self.below = Bulk(copies, tile, ext.at[:, END, TOP], (up, col))
        self.right = Bulk(copies, tile, ext.at[:, TOP, END], (row, left))
        corner = ext.at[:, END, END]
        self.diag = Bulk(copies, tile, corner, (up, left))
        self.onward, _ = copies.make(
            ext.at[:, END, TOP], corner, (row, left), self.diag.k
        )

    def start_sides(self, first=0, stop=4):
        self.right.start(first, stop)

        @pl.when(self.core == 0)
        def _():
            self.diag.start(first, stop)

    def finish(self):
        self.below.whole.wait_recv()

        @pl.when(self.core == 1)
        def _():
            self.onward.start()

        self.below.whole.wait_send()
        self.right.whole.wait()
        self.onward.wait()


def start_kernel(obj_ref, amps_ref, ext_ref, all_ref, send_sem, recv_sem, own_sem):
    row, col, z, y, x, core, device = whereabouts()
    left, right, up, down = around(row, col)
    twin = device(z, y, x, 1 - core)
    beside = device(z, y + 1 - 2 * (y % 2), x, core)
    ahead, behind = device(z, y, (x + 1) % 4, core), device(z, y, (x + 3) % 4, core)
    freer = device(z, y, (x + 1 + 2 * (y % 2)) % 4, core)
    greet(
        [
            twin,
            beside,
            ahead,
            behind,
            (row, left),
            (row, right),
            (up, col),
            (down, col),
            (up, left),
            (down, right),
        ]
    )
    copies = Copies(send_sem, recv_sem)

    def block(x, ylo, first=0, count=4):
        c = (x % 4) * 4 + ylo * 2 + core
        return all_ref.at[pl.ds(c * 4 + first, count)]

    ylo = y % 2
    mine, other = block(x, ylo), block(x, 1 - ylo)
    to_beside = copies.send(amps_ref, mine, beside)
    to_ahead = copies.send(amps_ref, mine, ahead)
    to_behind = copies.send(amps_ref, mine, behind)
    halo = Halo(copies, obj_ref, ext_ref, row, col, core)
    own = [
        pltpu.make_async_copy(amps_ref, mine, own_sem.at[0]),
        pltpu.make_async_copy(obj_ref, ext_ref.at[:, TOP, TOP], own_sem.at[1]),
    ]
    for copy in own:
        copy.start()
    rest = [copies.send(amps_ref, mine, twin)]
    to_beside.wait_recv()
    ahead_2 = copies.send(other, other, ahead)
    behind_2 = copies.send(other, other, behind)
    halo.below.start()
    halo.start_sides()
    rest.append(copies.send(other, other, twin))
    far = []
    for low, high, side in ((to_ahead, to_behind, ylo), (ahead_2, behind_2, 1 - ylo)):
        low.wait_recv()
        part = block(x + 3, side, 0, 2)
        far.append((copies.send(part, part, ahead), block(x + 2, side, 0, 2)))
        whole = block(x + 3, side)
        rest.append(copies.send(whole, whole, twin))
        high.wait_recv()
        part = block(x + 1, side, 3, 1)
        far.append((copies.send(part, part, behind), block(x + 2, side, 3, 1)))
        part = block(x + 3 - 2 * ylo, side, 2, 1)
        far.append((copies.send(part, part, freer), block(x + 2, side, 2, 1)))
        whole = block(x + 1, side)
        rest.append(copies.send(whole, whole, twin))
    for copy, part in far:
        copy.wait_recv()
        rest.append(copies.send(part, part, twin))
    for copy in own:
        copy.wait()
    for copy in (to_beside, to_ahead, to_behind, ahead_2, behind_2):
        copy.wait_send()
    for copy, _ in far:
        copy.wait_send()
    for copy in rest:
        copy.wait()
    halo.finish()


def run_start(obj, amplitudes):
    count = 3 + 2 + 3 + 12 + 6
    return pl.pallas_call(
        start_kernel,
        out_shape=(
            jax.ShapeDtypeStruct((2, 2 * N, 2 * N), jnp.float32),
            jax.ShapeDtypeStruct((64, N, N), jnp.bfloat16),
        ),
        in_specs=[VMEM, ANY],
        out_specs=(VMEM, ANY),
        scratch_shapes=[
            pltpu.SemaphoreType.DMA((count,)),
            pltpu.SemaphoreType.DMA((count,)),
            pltpu.SemaphoreType.DMA((2,)),
        ],
        compiler_params=pltpu.CompilerParams(
            collective_id=1, has_side_effects=True, vmem_limit_bytes=16 * 2**20
        ),
        name="start",
    )(obj, amplitudes)


def exchange_kernel(
    last,
    sums_ref,
    near_ref,
    ext_ref,
    part_ref,
    old_ref,
    tile_ref,
    out_ref,
    from_left,
    from_above,
    corner,
    low,
    pair,
    half,
    from_x,
    quarter,
    from_z,
    small,
    from_y,
    weights,
    power_high,
    power_low,
    send_sem,
    recv_sem,
):
    row, col, z, y, x, core, device = whereabouts()
    left, right, up, down = around(row, col)
    twin = device(z, y, x, 1 - core)
    on_x = [device(z, y, (x + d) % 4, core) for d in (1, 2, 3)]
    on_y = [device(z, (y + d) % 4, x, core) for d in (1, 2, 3)]
    on_z = [device((z + d) % 4, y, x, core) for d in (1, 2, 3)]
    greet(
        [
            (row, left),
            (row, right),
            (up, col),
            (down, col),
            (up, left),
            (down, right),
            twin,
            *on_x,
            *on_y,
            *on_z,
        ]
    )
    copies = Copies(send_sem, recv_sem)

    def finish(group):
        for copy in group:
            copy.wait()

    def add_weights(start, stop):
        gap = lax.broadcasted_iota(jnp.int32, (N, N), 0) - lax.broadcasted_iota(
            jnp.int32, (N, N), 1
        )

        def add(i, _):
            dy, dx = near_ref[2 * i], near_ref[2 * i + 1]
            to_row = jnp.where(gap == dy, 1.0, 0.0).astype(jnp.bfloat16)
            to_col = jnp.where(gap == -dx, 1.0, 0.0).astype(jnp.bfloat16)
            a = mm(power_high[...], to_col).astype(jnp.bfloat16)
            b = mm(power_low[...], to_col).astype(jnp.bfloat16)
            weights[...] += mm(to_row, a) + mm(to_row, b)
            return 0

        lax.fori_loop(start, stop, add, 0, unroll=4)

    on_pair = copies.send(part_ref.at[:, 1 - core], pair, twin)
    edge = sums_ref.at[:, END, END]
    inside, k = copies.make(edge, corner, twin)
    outside = Bulk(copies, edge, corner, (down, right), k)
    down_sums = Bulk(copies, sums_ref.at[:, END, TOP], from_above, (down, col))
    down_joint = Bulk(copies, low, from_above, (down, col), down_sums.k)
    to_right = Bulk(copies, sums_ref.at[:, TOP, END], from_left, (row, right))

    def send_down(first, stop):
        @pl.when(core == 0)
        def _():
            down_sums.start(first, stop)

        @pl.when(core == 1)
        def _():
            down_joint.start(first, stop)

    def send_right(first, stop):
        @pl.when(core == 1)
        def _():
            outside.start(first, stop)

        to_right.start(first, stop)

    @pl.when(core == 0)
    def _():
        inside.start()

    weights[...] = jnp.zeros((N, N), jnp.float32)
    for k in range(2):
        cols = pl.ds(k * H, H)
        power = old_ref[0, k] * old_ref[0, k] + old_ref[1, k] * old_ref[1, k]
        power_high[:, cols], power_low[:, cols] = split(power)
    on_pair.wait()
    for q in range(3):
        half[q] = part_ref[q, core] + pair[q]
    group = [
        copies.send(
            half.at[:, pl.ds(pl.multiple_of((x + d) % 4 * 64, 64), 64), :],
            from_x.at[d - 1],
            on_x[d - 1],
        )
        for d in (1, 2, 3)
    ]

    @pl.when(core == 1)
    def _():
        inside.wait_recv()
        low[...] = sums_ref[:, END, TOP] + corner[...]

    send_down(0, 2)
    add_weights(0, 16)
    finish(group)
    mine = pl.ds(pl.multiple_of(x * 64, 64), 64)
    quarter[...] = (half[:, mine, :] + from_x[0]) + (from_x[1] + from_x[2])
    group = [
        copies.send(
            quarter.at[:, pl.ds(pl.multiple_of((z + d) % 4 * 16, 16), 16), :],
            from_z.at[d - 1],
            on_z[d - 1],
        )
        for d in (1, 2, 3)
    ]

    send_right(0, 2)
    add_weights(16, 24)
    finish(group)
    mine = pl.ds(pl.multiple_of(z * 16, 16), 16)
    small[...] = (quarter[:, mine, :] + from_z[0]) + (from_z[1] + from_z[2])
    group = [copies.send(small, from_y.at[y], peer) for peer in on_y]
    from_y[y] = small[...]
    send_down(2, 4)
    send_right(2, 4)
    add_weights(24, 32)

    def object_update():
        to_right.whole.wait()
        down_sums.whole.wait()

        @pl.when(core == 0)
        def _():
            outside.whole.wait_recv()

        outside.whole.wait_send()
        for r in range(0, N, STRIP):
            rows = pl.ds(r, STRIP)
            scale = 1.0 / (weights[rows, :] + object_regular)
            for q in range(2):
                total = sums_ref[q, rows, TOP] + from_left[q, rows, :]
                total = total + from_above[q, rows, :]
                total = total + jnp.where(core == 0, corner[q, rows, :], 0.0)
                tile_ref[q, rows, TOP] = ext_ref[q, rows, TOP] + total * scale

    finish(group)
    total = (from_y[0] + from_y[1]) + (from_y[2] + from_y[3])
    rows = pl.ds(pl.multiple_of(x * 64 + z * 16, 16), 16)
    for q in range(2):
        out_ref[q, core, rows, :] = old_ref[q, core, rows, :] + total[q] / (
            total[2] + probe_regular
        )
    piece = out_ref.at[:, core, rows, :]
    group = [copies.send(piece, piece, peer) for peer in on_z]
    if not last:
        object_update()
        halo = Halo(copies, tile_ref.at[:, TOP, TOP], tile_ref, row, col, core)
        halo.below.start()
    finish(group)
    piece = out_ref.at[:, core, pl.ds(pl.multiple_of(x * 64, 64), 64), :]
    group = [copies.send(piece, piece, peer) for peer in on_x]
    finish(group)
    if not last:
        halo.start_sides()
    piece = out_ref.at[:, core]
    to_twin = copies.send(piece, piece, twin)
    if last:
        object_update()
    else:
        halo.finish()
    to_twin.wait()


def run_exchange(last, sums, near, ext, partials, probe):
    f32 = jnp.float32
    count = 4 + 9 + (0 if last else 3) + 7
    tile = (2, N, N) if last else (2, 2 * N, 2 * N)
    return pl.pallas_call(
        functools.partial(exchange_kernel, last),
        out_shape=(
            jax.ShapeDtypeStruct(tile, f32),
            jax.ShapeDtypeStruct((2, 2, N, H), f32),
        ),
        in_specs=[VMEM, SMEM, VMEM, VMEM, VMEM],
        out_specs=(VMEM, VMEM),
        scratch_shapes=[
            pltpu.VMEM((2, N, N), f32),
            pltpu.VMEM((2, N, N), f32),
            pltpu.VMEM((2, N, N), f32),
            pltpu.VMEM((2, N, N), f32),
            pltpu.VMEM((3, N, H), f32),
            pltpu.VMEM((3, N, H), f32),
            pltpu.VMEM((3, 3, 64, H), f32),
            pltpu.VMEM((3, 64, H), f32),
            pltpu.VMEM((3, 3, 16, H), f32),
            pltpu.VMEM((3, 16, H), f32),
            pltpu.VMEM((4, 3, 16, H), f32),
            pltpu.VMEM((N, N), f32),
            pltpu.VMEM((N, N), jnp.bfloat16),
            pltpu.VMEM((N, N), jnp.bfloat16),
            pltpu.SemaphoreType.DMA((count,)),
            pltpu.SemaphoreType.DMA((count,)),
        ],
        compiler_params=pltpu.CompilerParams(
            collective_id=3 if last else 2,
            has_side_effects=True,
            vmem_limit_bytes=14 * 2**20,
        ),
        name="finish" if last else "exchange",
    )(sums, near, ext, partials, probe)


def local(obj, probe, amplitudes, positions):
    place = jnp.stack([lax.axis_index("row"), lax.axis_index("col")]).astype(jnp.int32)
    pos = positions.reshape(-1)
    high, low = real_tables()
    sel = order_tables()
    illum = jnp.stack([probe[:, :, :H], probe[:, :, H:]], axis=1)
    ext, gathered = run_start(obj, amplitudes)
    near = None
    for sweep in range(ITERS):
        sums, partials, listed = run_patterns(
            sweep == 0, pos, place, ext, illum, gathered, high, low, sel
        )
        near = listed if sweep == 0 else near
        ext, illum = run_exchange(
            sweep == ITERS - 1, sums, near, ext, partials, illum
        )
    return ext, jnp.concatenate([illum[:, 0], illum[:, 1]], axis=2)


def solution(mesh):
    placed = (P(None, "row", "col"), P(), P(("row", "col"), None, None), P())
    return jax.shard_map(
        local,
        mesh=mesh,
        in_specs=placed,
        out_specs=(P(None, "row", "col"), P()),
        check_vma=False,
    )
```

```python
import functools

import jax
import jax.numpy as jnp
import numpy as np
from jax import lax
from jax.experimental import pallas as pl
from jax.experimental.pallas import tpu as pltpu
from jax.sharding import PartitionSpec as P

ITERS = 2
amplitude_floor = 0.1
object_regular = 0.5
probe_regular = 1.0

N = 256
NEAR = 32
FAR = 4096
H = 128
STRIP = 32


def real_tables():
    n = np.arange(H)
    out = []
    for odd in (0, 1):
        phase = (n[:, None] * (2 * n[None, :] + odd)) % N
        angle = phase * (2 * np.pi / N)
        re, im = np.cos(angle) / 16.0, -np.sin(angle) / 16.0
        full = np.block([[re, im], [-im, re]]).astype(np.float32)
        out += [full, full.T]
    full = jnp.asarray(np.stack(out))
    high = full.astype(jnp.bfloat16)
    low = (full - high.astype(jnp.float32)).astype(jnp.bfloat16)
    return high, low


def order_tables():
    order = np.concatenate([np.arange(0, N, 2), np.arange(1, N, 2)])
    sel = np.zeros((N, N), np.float32)
    sel[np.arange(N), order] = 1.0
    return jnp.asarray(np.stack([sel, sel.T])).astype(jnp.bfloat16)


def split(x):
    high = x.astype(jnp.bfloat16)
    low = (x - high.astype(jnp.float32)).astype(jnp.bfloat16)
    return high, low


def mm(a, b):
    return jnp.dot(a, b, preferred_element_type=jnp.float32)


def pattern_kernel(
    first,
    pos_ref,
    place_ref,
    ext,
    probe_ref,
    amps_ref,
    th_ref,
    tl_ref,
    sel_ref,
    sums_ref,
    part_ref,
    near_ref,
    todo,
    *work,
):
    band = place_ref[0]
    my_col = place_ref[1]
    for r in range(0, 2 * N, STRIP):
        for q in range(2):
            sums_ref[q, pl.ds(r, STRIP), :] = jnp.zeros((STRIP, 2 * N), jnp.float32)
    part_ref[...] = jnp.zeros_like(part_ref)

    lane = lax.broadcasted_iota(jnp.int32, (STRIP, H), 1)

    def process(spaces, j, top, left, valid):
        amp, win, psi, ah, al, ye, yo = spaces
        r8 = pl.multiple_of((top // 8) * 8, 8)
        dr = top - r8
        c128 = pl.multiple_of((left // H) * H, H)
        dc = left - c128

        def cut(s, _):
            r0 = s * STRIP
            w = []
            for q in range(2):
                block = ext[q, pl.ds(r8 + r0, STRIP + 8), pl.ds(c128, 3 * H)]
                block = pltpu.roll(block, lax.rem(STRIP + 8 - dr, STRIP + 8), 0)[:STRIP]
                turned = [
                    pltpu.roll(block[:, k * H : (k + 1) * H], lax.rem(H - dc, H), 1)
                    for k in range(3)
                ]
                keep = lane < H - dc
                w.append(
                    [
                        jnp.where(keep, turned[0], turned[1]),
                        jnp.where(keep, turned[1], turned[2]),
                    ]
                )
            rows = pl.ds(r0, STRIP)
            x = []
            for k in range(2):
                cols = pl.ds(k * H, H)
                wr, wi = w[0][k], w[1][k]
                win[0, rows, cols] = wr
                win[1, rows, cols] = wi
                pr, pi = probe_ref[0, k, rows, :], probe_ref[1, k, rows, :]
                er = pr * wr - pi * wi
                ei = pr * wi + pi * wr
                psi[0, rows, cols] = er
                psi[1, rows, cols] = ei
                x.append((er, ei))
            for k, z in enumerate(
                (
                    x[0][0] + x[1][0],
                    x[0][1] + x[1][1],
                    x[0][0] - x[1][0],
                    x[0][1] - x[1][1],
                )
            ):
                high, low = split(z)
                ah[k // 2, rows, pl.ds((k % 2) * H, H)] = high
                al[k // 2, rows, pl.ds((k % 2) * H, H)] = low
            return 0

        for s in range(N // STRIP):
            cut(s, 0)
        yield

        def right_apply(t):
            for k, out in ((0, ye), (1, yo)):
                th, tl = th_ref[2 * k + t], tl_ref[2 * k + t]
                out[...] = mm(ah[k], th) + mm(al[k], th) + mm(ah[k], tl)

        def left_apply(t):
            for k, out in ((0, ye), (1, yo)):
                th, tl = th_ref[2 * k + t], tl_ref[2 * k + t]
                out[...] = mm(th, ah[k]) + mm(th, al[k]) + mm(tl, ah[k])

        def put(k, rows, cols, z):
            high, low = split(z)
            ah[k, rows, cols] = high
            al[k, rows, cols] = low

        right_apply(0)
        yield

        def rows_forward(s, _):
            r0 = s * STRIP
            up, down = pl.ds(r0, STRIP), pl.ds(r0 + H, STRIP)
            for k, src in ((0, ye), (1, yo)):
                cols = pl.ds(k * H, H)
                for q in range(2):
                    part = pl.ds(q * H, H)
                    a, b = src[up, part], src[down, part]
                    dest = up if q == 0 else down
                    put(0, dest, cols, a + b)
                    put(1, dest, cols, a - b)
            return 0

        for s in range(H // STRIP):
            rows_forward(s, 0)
        yield
        left_apply(1)
        amp[...] = mm(mm(sel_ref[0], amps_ref[j]).astype(jnp.bfloat16), sel_ref[1])
        yield

        def modulus(s, _):
            r0 = s * STRIP
            up, down = pl.ds(r0, STRIP), pl.ds(r0 + H, STRIP)
            for k, src in ((0, ye), (1, yo)):
                re, im = src[up, :], src[down, :]
                m = amp[pl.ds(r0 + k * H, STRIP), :]
                f = m * lax.rsqrt(re * re + im * im + amplitude_floor)
                put(k, up, slice(None), re * f)
                put(k, down, slice(None), im * f)
            return 0

        for s in range(H // STRIP):
            modulus(s, 0)
        yield
        left_apply(0)
        yield

        def rows_back(s, _):
            r0 = s * STRIP
            up, down = pl.ds(r0, STRIP), pl.ds(r0 + H, STRIP)
            for q, src_rows in ((0, up), (1, down)):
                part = pl.ds(q * H, H)
                e, o = ye[src_rows, :], yo[src_rows, :]
                for dest, z in ((up, e + o), (down, e - o)):
                    put(0, dest, part, z[:, :H])
                    put(1, dest, part, z[:, H:])
            return 0

        for s in range(H // STRIP):
            rows_back(s, 0)
        yield
        right_apply(1)
        yield

        def finish(s, _):
            r0 = s * STRIP
            rows = pl.ds(r0, STRIP)
            e_re, e_im = ye[rows, :H], ye[rows, H:]
            o_re, o_im = yo[rows, :H], yo[rows, H:]
            term = [[], []]
            for k in range(2):
                cols = pl.ds(k * H, H)
                br = e_re + o_re if k == 0 else e_re - o_re
                bi = e_im + o_im if k == 0 else e_im - o_im
                cr = (br - psi[0, rows, cols]) * valid
                ci = (bi - psi[1, rows, cols]) * valid
                pr, pi = probe_ref[0, k, rows, :], probe_ref[1, k, rows, :]
                wr, wi = win[0, rows, cols], win[1, rows, cols]
                term[0].append(pr * cr + pi * ci)
                term[1].append(pr * ci - pi * cr)
                part_ref[0, k, rows, :] += wr * cr + wi * ci
                part_ref[1, k, rows, :] += wr * ci - wi * cr
                part_ref[2, k, rows, :] += (wr * wr + wi * wi) * valid
            for q in range(2):
                deposit(sums_ref.at[q], r8 + r0, c128, dr, dc, lane, term[q])
            return 0

        for s in range(N // STRIP):
            finish(s, 0)
        yield

    def visit(i, found):
        j = band * 64 + i
        mine = pos_ref[2 * j + 1] // N == my_col

        @pl.when(mine)
        def _():
            todo[found] = i

        return found + mine.astype(jnp.int32)

    count = lax.fori_loop(0, 64, visit, 0)

    def pair(k, _):
        lanes = []
        for half in range(2):
            at = 2 * k + half
            i = todo[jnp.minimum(at, count - 1)]
            j = band * 64 + i
            valid = (at < count).astype(jnp.float32)
            lanes.append(
                process(
                    work[7 * half : 7 * half + 7],
                    i,
                    pos_ref[2 * j] - band * N,
                    pos_ref[2 * j + 1] - my_col * N,
                    valid,
                )
            )
        next(lanes[0])
        alive = [True, True]
        while any(alive):
            for half in (1, 0):
                if alive[half]:
                    alive[half] = next(lanes[half], 0) is None
        return 0

    lax.fori_loop(0, (count + 1) // 2, pair, 0)
    if not first:
        return

    for k in range(2 * NEAR):
        near_ref[k] = FAR

    def note(j, found):
        dy = pos_ref[2 * j] - band * N
        dx = pos_ref[2 * j + 1] - my_col * N
        reach = (dy > -N) & (dx > -N) & (dy < N) & (dx < N)

        @pl.when(reach)
        def _():
            near_ref[2 * found] = dy
            near_ref[2 * found + 1] = dx

        return found + reach.astype(jnp.int32)

    lax.fori_loop(jnp.maximum(band - 1, 0) * 64, (band + 1) * 64, note, 0)


def deposit(sums, row, col, dr, dc, lane, halves):
    a, b = (pltpu.roll(z, dc, 1) for z in halves)
    hold = lane < dc
    zero = jnp.zeros_like(a)
    wide = jnp.concatenate(
        [jnp.where(hold, zero, a), jnp.where(hold, a, b), jnp.where(hold, b, zero)],
        axis=1,
    )
    tall = jnp.concatenate([wide, jnp.zeros((8, 3 * H), jnp.float32)], axis=0)
    tall = pltpu.roll(tall, dr, 0)
    spot = (pl.ds(pl.multiple_of(row, 8), STRIP + 8), pl.ds(col, 3 * H))
    sums[spot] = sums[spot] + tall


SMEM = pl.BlockSpec(memory_space=pltpu.SMEM)
VMEM = pl.BlockSpec(memory_space=pltpu.VMEM)
ANY = pl.BlockSpec(memory_space=pltpu.HBM)


def run_patterns(first, pos, place, ext, probe, gathered, high, low, sel):
    f32, bf16 = jnp.float32, jnp.bfloat16
    return pl.pallas_call(
        functools.partial(pattern_kernel, first),
        out_shape=(
            jax.ShapeDtypeStruct((2, 2 * N, 2 * N), f32),
            jax.ShapeDtypeStruct((3, 2, N, H), f32),
            jax.ShapeDtypeStruct((2 * NEAR,), jnp.int32),
        ),
        in_specs=[SMEM, SMEM, VMEM, VMEM, VMEM, VMEM, VMEM, VMEM],
        out_specs=(VMEM, VMEM, SMEM),
        scratch_shapes=[
            pltpu.SMEM((64,), jnp.int32),
            *2
            * (
                pltpu.VMEM((N, N), f32),
                pltpu.VMEM((2, N, N), f32),
                pltpu.VMEM((2, N, N), f32),
                pltpu.VMEM((2, N, N), bf16),
                pltpu.VMEM((2, N, N), bf16),
                pltpu.VMEM((N, N), f32),
                pltpu.VMEM((N, N), f32),
            ),
        ],
        compiler_params=pltpu.CompilerParams(vmem_limit_bytes=24 * 2**20),
        name="patterns",
    )(pos, place, ext, probe, gathered, high, low, sel)


MESH = pl.DeviceIdType.MESH


def whereabouts():
    row, col = lax.axis_index("row"), lax.axis_index("col")
    z, y = row // 2, (row % 2) * 2 + (col // 2) % 2
    x, core = col // 4, col % 2

    def device(z, y, x, core):
        return (z * 2 + y // 2, x * 4 + (y % 2) * 2 + core)

    return row, col, z, y, x, core, device


def greet(peers):
    barrier = pltpu.get_barrier_semaphore()
    for peer in peers:
        pl.semaphore_signal(barrier, inc=1, device_id=peer, device_id_type=MESH)
    pl.semaphore_wait(barrier, len(peers))


class Copies:
    def __init__(self, send_sem, recv_sem):
        self.send_sem, self.recv_sem, self.made = send_sem, recv_sem, []

    def make(self, src, dst, peer, k=None):
        if k is None:
            k = len(self.made)
            self.made.append(None)
        copy = pltpu.make_async_remote_copy(
            src_ref=src,
            dst_ref=dst,
            send_sem=self.send_sem.at[k],
            recv_sem=self.recv_sem.at[k],
            device_id=peer,
            device_id_type=MESH,
        )
        self.made[k] = copy
        return copy, k

    def send(self, src, dst, peer):
        copy, _ = self.make(src, dst, peer)
        copy.start()
        return copy


def around(row, col):
    left, right = lax.rem(col + 15, 16), lax.rem(col + 1, 16)
    up, down = lax.rem(row + 7, 8), lax.rem(row + 1, 8)
    return left, right, up, down


TOP, END = slice(0, N), slice(N, 2 * N)


class Bulk:
    def __init__(self, copies, src, dst, peer, k=None):
        self.whole, self.k = copies.make(src, dst, peer, k)
        self.copies, self.src, self.dst, self.peer = copies, src, dst, peer

    def start(self, first=0, stop=4):
        for part in range(first, stop):
            rows = pl.ds(part * 64, 64)
            self.copies.make(
                self.src.at[:, rows], self.dst.at[:, rows], self.peer, self.k
            )[0].start()


class Halo:
    def __init__(self, copies, tile, ext, row, col, core):
        left, right, up, down = around(row, col)
        self.core = core
        self.below = Bulk(copies, tile, ext.at[:, END, TOP], (up, col))
        self.right = Bulk(copies, tile, ext.at[:, TOP, END], (row, left))
        corner = ext.at[:, END, END]
        self.diag = Bulk(copies, tile, corner, (up, left))
        self.onward, _ = copies.make(
            ext.at[:, END, TOP], corner, (row, left), self.diag.k
        )

    def start_sides(self, first=0, stop=4):
        self.right.start(first, stop)

        @pl.when(self.core == 0)
        def _():
            self.diag.start(first, stop)

    def finish(self):
        self.below.whole.wait_recv()

        @pl.when(self.core == 1)
        def _():
            self.onward.start()

        self.below.whole.wait_send()
        self.right.whole.wait()
        self.onward.wait()


def start_kernel(obj_ref, amps_ref, ext_ref, all_ref, send_sem, recv_sem, own_sem):
    row, col, z, y, x, core, device = whereabouts()
    left, right, up, down = around(row, col)
    twin = device(z, y, x, 1 - core)
    beside = device(z, y + 1 - 2 * (y % 2), x, core)
    ahead, behind = device(z, y, (x + 1) % 4, core), device(z, y, (x + 3) % 4, core)
    freer = device(z, y, (x + 1 + 2 * (y % 2)) % 4, core)
    greet(
        [
            twin,
            beside,
            ahead,
            behind,
            (row, left),
            (row, right),
            (up, col),
            (down, col),
            (up, left),
            (down, right),
        ]
    )
    copies = Copies(send_sem, recv_sem)

    def block(x, ylo, first=0, count=4):
        c = (x % 4) * 4 + ylo * 2 + core
        return all_ref.at[pl.ds(c * 4 + first, count)]

    ylo = y % 2
    mine, other = block(x, ylo), block(x, 1 - ylo)
    to_beside = copies.send(amps_ref, mine, beside)
    to_ahead = copies.send(amps_ref, mine, ahead)
    to_behind = copies.send(amps_ref, mine, behind)
    halo = Halo(copies, obj_ref, ext_ref, row, col, core)
    own = [
        pltpu.make_async_copy(amps_ref, mine, own_sem.at[0]),
        pltpu.make_async_copy(obj_ref, ext_ref.at[:, TOP, TOP], own_sem.at[1]),
    ]
    for copy in own:
        copy.start()
    rest = [copies.send(amps_ref, mine, twin)]
    to_beside.wait_recv()
    ahead_2 = copies.send(other, other, ahead)
    behind_2 = copies.send(other, other, behind)
    halo.below.start()
    halo.start_sides()
    rest.append(copies.send(other, other, twin))
    far = []
    for low, high, side in ((to_ahead, to_behind, ylo), (ahead_2, behind_2, 1 - ylo)):
        low.wait_recv()
        part = block(x + 3, side, 0, 2)
        far.append((copies.send(part, part, ahead), block(x + 2, side, 0, 2)))
        whole = block(x + 3, side)
        rest.append(copies.send(whole, whole, twin))
        high.wait_recv()
        part = block(x + 1, side, 3, 1)
        far.append((copies.send(part, part, behind), block(x + 2, side, 3, 1)))
        part = block(x + 3 - 2 * ylo, side, 2, 1)
        far.append((copies.send(part, part, freer), block(x + 2, side, 2, 1)))
        whole = block(x + 1, side)
        rest.append(copies.send(whole, whole, twin))
    for copy, part in far:
        copy.wait_recv()
        rest.append(copies.send(part, part, twin))
    for copy in own:
        copy.wait()
    for copy in (to_beside, to_ahead, to_behind, ahead_2, behind_2):
        copy.wait_send()
    for copy, _ in far:
        copy.wait_send()
    for copy in rest:
        copy.wait()
    halo.finish()


def run_start(obj, amplitudes):
    count = 3 + 2 + 3 + 12 + 6
    return pl.pallas_call(
        start_kernel,
        out_shape=(
            jax.ShapeDtypeStruct((2, 2 * N, 2 * N), jnp.float32),
            jax.ShapeDtypeStruct((64, N, N), jnp.bfloat16),
        ),
        in_specs=[VMEM, ANY],
        out_specs=(VMEM, ANY),
        scratch_shapes=[
            pltpu.SemaphoreType.DMA((count,)),
            pltpu.SemaphoreType.DMA((count,)),
            pltpu.SemaphoreType.DMA((2,)),
        ],
        compiler_params=pltpu.CompilerParams(
            collective_id=1, has_side_effects=True, vmem_limit_bytes=16 * 2**20
        ),
        name="start",
    )(obj, amplitudes)


def exchange_kernel(
    last,
    sums_ref,
    near_ref,
    ext_ref,
    part_ref,
    old_ref,
    tile_ref,
    out_ref,
    from_left,
    from_above,
    corner,
    low,
    pair,
    half,
    from_x,
    quarter,
    from_z,
    small,
    from_y,
    weights,
    power_high,
    power_low,
    send_sem,
    recv_sem,
):
    row, col, z, y, x, core, device = whereabouts()
    left, right, up, down = around(row, col)
    twin = device(z, y, x, 1 - core)
    on_x = [device(z, y, (x + d) % 4, core) for d in (1, 2, 3)]
    on_y = [device(z, (y + d) % 4, x, core) for d in (1, 2, 3)]
    on_z = [device((z + d) % 4, y, x, core) for d in (1, 2, 3)]
    greet(
        [
            (row, left),
            (row, right),
            (up, col),
            (down, col),
            (up, left),
            (down, right),
            twin,
            *on_x,
            *on_y,
            *on_z,
        ]
    )
    copies = Copies(send_sem, recv_sem)

    def finish(group):
        for copy in group:
            copy.wait()

    def add_weights(start, stop):
        gap = lax.broadcasted_iota(jnp.int32, (N, N), 0) - lax.broadcasted_iota(
            jnp.int32, (N, N), 1
        )

        def add(i, _):
            dy, dx = near_ref[2 * i], near_ref[2 * i + 1]
            to_row = jnp.where(gap == dy, 1.0, 0.0).astype(jnp.bfloat16)
            to_col = jnp.where(gap == -dx, 1.0, 0.0).astype(jnp.bfloat16)
            a = mm(power_high[...], to_col).astype(jnp.bfloat16)
            b = mm(power_low[...], to_col).astype(jnp.bfloat16)
            weights[...] += mm(to_row, a) + mm(to_row, b)
            return 0

        lax.fori_loop(start, stop, add, 0, unroll=4)

    on_pair = copies.send(part_ref.at[:, 1 - core], pair, twin)
    edge = sums_ref.at[:, END, END]
    inside, k = copies.make(edge, corner, twin)
    outside = Bulk(copies, edge, corner, (down, right), k)
    down_sums = Bulk(copies, sums_ref.at[:, END, TOP], from_above, (down, col))
    down_joint = Bulk(copies, low, from_above, (down, col), down_sums.k)
    to_right = Bulk(copies, sums_ref.at[:, TOP, END], from_left, (row, right))

    def send_down(first, stop):
        @pl.when(core == 0)
        def _():
            down_sums.start(first, stop)

        @pl.when(core == 1)
        def _():
            down_joint.start(first, stop)

    def send_right(first, stop):
        @pl.when(core == 1)
        def _():
            outside.start(first, stop)

        to_right.start(first, stop)

    @pl.when(core == 0)
    def _():
        inside.start()

    weights[...] = jnp.zeros((N, N), jnp.float32)
    for k in range(2):
        cols = pl.ds(k * H, H)
        power = old_ref[0, k] * old_ref[0, k] + old_ref[1, k] * old_ref[1, k]
        power_high[:, cols], power_low[:, cols] = split(power)
    on_pair.wait()
    for q in range(3):
        half[q] = part_ref[q, core] + pair[q]
    group = [
        copies.send(
            half.at[:, pl.ds(pl.multiple_of((x + d) % 4 * 64, 64), 64), :],
            from_x.at[d - 1],
            on_x[d - 1],
        )
        for d in (1, 2, 3)
    ]

    @pl.when(core == 1)
    def _():
        inside.wait_recv()
        low[...] = sums_ref[:, END, TOP] + corner[...]

    send_down(0, 2)
    add_weights(0, 16)
    finish(group)
    mine = pl.ds(pl.multiple_of(x * 64, 64), 64)
    quarter[...] = (half[:, mine, :] + from_x[0]) + (from_x[1] + from_x[2])
    group = [
        copies.send(
            quarter.at[:, pl.ds(pl.multiple_of((z + d) % 4 * 16, 16), 16), :],
            from_z.at[d - 1],
            on_z[d - 1],
        )
        for d in (1, 2, 3)
    ]

    send_right(0, 2)
    add_weights(16, 24)
    finish(group)
    mine = pl.ds(pl.multiple_of(z * 16, 16), 16)
    small[...] = (quarter[:, mine, :] + from_z[0]) + (from_z[1] + from_z[2])
    group = [copies.send(small, from_y.at[y], peer) for peer in on_y]
    from_y[y] = small[...]
    send_down(2, 4)
    send_right(2, 4)
    add_weights(24, 32)

    def object_update():
        to_right.whole.wait()
        down_sums.whole.wait()

        @pl.when(core == 0)
        def _():
            outside.whole.wait_recv()

        outside.whole.wait_send()
        for r in range(0, N, STRIP):
            rows = pl.ds(r, STRIP)
            scale = 1.0 / (weights[rows, :] + object_regular)
            for q in range(2):
                total = sums_ref[q, rows, TOP] + from_left[q, rows, :]
                total = total + from_above[q, rows, :]
                total = total + jnp.where(core == 0, corner[q, rows, :], 0.0)
                tile_ref[q, rows, TOP] = ext_ref[q, rows, TOP] + total * scale

    finish(group)
    total = (from_y[0] + from_y[1]) + (from_y[2] + from_y[3])
    rows = pl.ds(pl.multiple_of(x * 64 + z * 16, 16), 16)
    for q in range(2):
        out_ref[q, core, rows, :] = old_ref[q, core, rows, :] + total[q] / (
            total[2] + probe_regular
        )
    piece = out_ref.at[:, core, rows, :]
    group = [copies.send(piece, piece, peer) for peer in on_z]
    if not last:
        object_update()
        halo = Halo(copies, tile_ref.at[:, TOP, TOP], tile_ref, row, col, core)
        halo.below.start(0, 2)
    finish(group)
    piece = out_ref.at[:, core, pl.ds(pl.multiple_of(x * 64, 64), 64), :]
    group = [copies.send(piece, piece, peer) for peer in on_x]
    if not last:
        halo.below.start(2, 4)
    finish(group)
    if not last:
        halo.start_sides()
    piece = out_ref.at[:, core]
    to_twin = copies.send(piece, piece, twin)
    if last:
        object_update()
    else:
        halo.finish()
    to_twin.wait()


def run_exchange(last, sums, near, ext, partials, probe):
    f32 = jnp.float32
    count = 4 + 9 + (0 if last else 3) + 7
    tile = (2, N, N) if last else (2, 2 * N, 2 * N)
    return pl.pallas_call(
        functools.partial(exchange_kernel, last),
        out_shape=(
            jax.ShapeDtypeStruct(tile, f32),
            jax.ShapeDtypeStruct((2, 2, N, H), f32),
        ),
        in_specs=[VMEM, SMEM, VMEM, VMEM, VMEM],
        out_specs=(VMEM, VMEM),
        scratch_shapes=[
            pltpu.VMEM((2, N, N), f32),
            pltpu.VMEM((2, N, N), f32),
            pltpu.VMEM((2, N, N), f32),
            pltpu.VMEM((2, N, N), f32),
            pltpu.VMEM((3, N, H), f32),
            pltpu.VMEM((3, N, H), f32),
            pltpu.VMEM((3, 3, 64, H), f32),
            pltpu.VMEM((3, 64, H), f32),
            pltpu.VMEM((3, 3, 16, H), f32),
            pltpu.VMEM((3, 16, H), f32),
            pltpu.VMEM((4, 3, 16, H), f32),
            pltpu.VMEM((N, N), f32),
            pltpu.VMEM((N, N), jnp.bfloat16),
            pltpu.VMEM((N, N), jnp.bfloat16),
            pltpu.SemaphoreType.DMA((count,)),
            pltpu.SemaphoreType.DMA((count,)),
        ],
        compiler_params=pltpu.CompilerParams(
            collective_id=3 if last else 2,
            has_side_effects=True,
            vmem_limit_bytes=14 * 2**20,
        ),
        name="finish" if last else "exchange",
    )(sums, near, ext, partials, probe)


def local(obj, probe, amplitudes, positions):
    place = jnp.stack([lax.axis_index("row"), lax.axis_index("col")]).astype(jnp.int32)
    pos = positions.reshape(-1)
    high, low = real_tables()
    sel = order_tables()
    illum = jnp.stack([probe[:, :, :H], probe[:, :, H:]], axis=1)
    ext, gathered = run_start(obj, amplitudes)
    near = None
    for sweep in range(ITERS):
        sums, partials, listed = run_patterns(
            sweep == 0, pos, place, ext, illum, gathered, high, low, sel
        )
        near = listed if sweep == 0 else near
        ext, illum = run_exchange(
            sweep == ITERS - 1, sums, near, ext, partials, illum
        )
    return ext, jnp.concatenate([illum[:, 0], illum[:, 1]], axis=2)


def solution(mesh):
    placed = (P(None, "row", "col"), P(), P(("row", "col"), None, None), P())
    return jax.shard_map(
        local,
        mesh=mesh,
        in_specs=placed,
        out_specs=(P(None, "row", "col"), P()),
        check_vma=False,
    )
```
